512 devices in a mesh: dp: 16 (over x, y), expert: 32 (over z, core).
Axes of the slice: x: 4, y: 4, z: 16, core: 2. Of those that a mesh axis runs over, the one named last changes fastest.
Arguments:
- out_grad: bfloat16 [65536, 5120], P(('dp', 'expert')), may hold values from -6 to 6
- route_ids: int32 [65536, 6], P(('dp', 'expert')), may hold values from 0 to 159, as said below
- route_slots: int32 [65536, 6], P(('dp', 'expert')), may hold values from 0 to 4, as said below
- route_probs: float32 [65536, 6], P(('dp', 'expert')), may hold values from 0.03 to 0.5
- saved_pre: bfloat16 [32, 2560, 1536], P('expert', 'dp'), may hold values from -8 to 8
- w_gate: bfloat16 [32, 5120, 768], P('expert', 'dp'), may hold values from -0.078125 to 0.078125
- w_up: bfloat16 [32, 5120, 768], P('expert', 'dp'), may hold values from -0.078125 to 0.078125
- w_down: bfloat16 [32, 768, 5120], P('expert', None, 'dp'), may hold values from -0.21875 to 0.21875
Outputs:
- input_grad: bfloat16 [65536, 5120], P(('dp', 'expert'))
- grad_down: bfloat16 [32, 768, 5120], P('expert', None, 'dp')
The draws below stay inside these ranges and needn't reach their ends.
Inputs may be any that keep to these rules, and one draw needn't show every extreme that they name: `route_ids`: each row names 6 different experts. Among the 128 rows of one device every expert is named between 4 and 5 times, and some expert exactly 5 times. `route_slots`: among the 128 rows of one device, the routes to one expert have distinct slots.
All inputs are finite; a program needn't handle non-finite values.
Results may differ from the reference program's by a relative error of at most 0.022.
Values may be sent and summed in bfloat16 or wider, within the bound.
No kernel may reach another device: no remote copies, remote signals or barrier semaphores. Data moves between devices by JAX's collectives and lax.ppermute only.
A program may use at most 128 MiB of HBM per device.

```python
import math
import jax
import jax.numpy as jnp
from jax import lax

D = 5120
FF = 768
TOPK = 6
TOK_DEV = 128
ALL_EXPERTS = 160
EXPERTS = 32
CAP = 5
SLOTS = 2560
TOKENS = 65536
N_DP = 16


def route_table(key):
    blocks = TOKENS // TOK_DEV
    first, second, third = jax.random.split(key, 3)
    token_perm = jax.vmap(lambda k: jax.random.permutation(k, TOK_DEV))(jax.random.split(first, blocks))
    expert_perm = jax.vmap(lambda k: jax.random.permutation(k, ALL_EXPERTS))(jax.random.split(second, blocks))
    slot_perm = jax.vmap(lambda k: jax.random.permutation(k, CAP))(jax.random.split(third, blocks * ALL_EXPERTS))
    slot_perm = slot_perm.reshape(blocks, ALL_EXPERTS * CAP)
    order = token_perm[:, :, None] * TOPK + jnp.arange(TOPK, dtype=jnp.int32)[None, None, :]
    column = (order % ALL_EXPERTS).reshape(blocks, TOK_DEV * TOPK)
    rank = (order // ALL_EXPERTS).reshape(blocks, TOK_DEV * TOPK)
    route_ids = jnp.take_along_axis(expert_perm, column, axis=1)
    route_slots = jnp.take_along_axis(slot_perm, column * CAP + rank, axis=1)
    return (route_ids.reshape(TOKENS, TOPK).astype(jnp.int32), route_slots.reshape(TOKENS, TOPK).astype(jnp.int32))


def draw_route_ids(key, part):
    route_ids, route_slots = route_table(key)
    return route_ids


def draw_route_slots(key, part):
    route_ids, route_slots = route_table(key)
    return route_slots


def block_scale(key, dims, cuts, smallest, largest):
    level, own = 1.0, jax.random.fold_in(key, 6)
    for dim, shards_of in cuts:
        draws = jnp.exp(jax.random.uniform(jax.random.fold_in(own, dim), (shards_of,), jnp.float32, smallest / len(cuts), largest / len(cuts)))
        level = level * jnp.repeat(draws, dims[dim] // shards_of).reshape([-1 if axis == dim else 1 for axis in range(len(dims))])
    return level


def scatter_about(key, extent, width, bound, pieces=(), held_as=jnp.bfloat16):
    factor_of = block_scale(key, extent, pieces, -0.22, 0.18) if pieces else 1.0
    array = jax.random.normal(key, extent, jnp.float32) * width * factor_of
    return jnp.minimum(jnp.maximum(array, -bound), bound).astype(held_as)


def setup_inputs(seed: int = 0) -> dict:
    key_list = jax.random.split(jax.random.key(seed), 9)
    out_grad = scatter_about(key_list[0], (TOKENS, D), 1.0, 6.0, ((0, 512),))
    route_ids = draw_route_ids(jax.random.fold_in(key_list[8], 71), 0)
    route_slots = draw_route_slots(jax.random.fold_in(key_list[8], 71), 0)
    route_probs = jnp.clip(jnp.exp(math.log(0.5) - 2.8134107 * jax.random.uniform(key_list[3], (TOKENS, TOPK), jnp.float32) ** block_scale(key_list[3], (TOKENS, TOPK), ((0, 512),), -0.2, 0.2)), 0.03, 0.5)
    saved_pre = scatter_about(key_list[4], (EXPERTS, SLOTS, 2 * FF), 1.5, 8.0, ((0, 32), (1, 16)))
    w_gate = scatter_about(key_list[5], (EXPERTS, D, FF), D ** -0.5, 0.078125, ((0, 32), (1, 16)))
    w_up = scatter_about(key_list[6], (EXPERTS, D, FF), D ** -0.5, 0.078125, ((0, 32), (1, 16)))
    w_down = scatter_about(key_list[7], (EXPERTS, FF, D), FF ** -0.5, 0.21875, ((0, 32), (2, 16)))
    return {"out_grad": out_grad, "route_ids": route_ids, "route_slots": route_slots, "route_probs": route_probs, "saved_pre": saved_pre, "w_gate": w_gate, "w_up": w_up, "w_down": w_down}


def reference(out_grad, route_ids, route_slots, route_probs, saved_pre, w_gate, w_up, w_down):
    token_index = jnp.arange(TOKENS, dtype=jnp.int32)
    slot_pos = ((token_index // TOK_DEV)[:, None] * CAP + route_slots).astype(jnp.int32)
    in_window = route_ids < EXPERTS
    safe_ids = jnp.where(in_window, route_ids, EXPERTS).astype(jnp.int32)
    owner = jnp.zeros((EXPERTS, SLOTS), jnp.int32).at[safe_ids, slot_pos].set(
        jnp.broadcast_to(token_index[:, None], route_ids.shape), mode="drop")
    scale_table = jnp.zeros((EXPERTS, SLOTS), jnp.float32).at[safe_ids, slot_pos].set(
        route_probs.astype(jnp.float32), mode="drop")
    slice_width = D // N_DP

    def per_expert(expert):
        sent = (scale_table[expert][:, None] * out_grad[owner[expert]].astype(jnp.float32)).astype(jnp.bfloat16)
        blocks_sent = sent.astype(jnp.float32).reshape(SLOTS, N_DP, slice_width)
        blocks_down = w_down[expert].astype(jnp.float32).reshape(FF, N_DP, slice_width)
        partials = jnp.einsum("snk,fnk->nsf", blocks_sent, blocks_down).astype(jnp.bfloat16)
        partials = lax.optimization_barrier(partials)
        hidden_grad = jnp.sum(partials.astype(jnp.float32), axis=0)
        pre = saved_pre[expert].astype(jnp.float32)
        gate_pre = pre[:, :FF]
        up_pre = pre[:, FF:]
        sig = jax.nn.sigmoid(gate_pre)
        lift = gate_pre * sig
        act = (lift * up_pre).astype(jnp.bfloat16)
        gate_grad = (hidden_grad * up_pre * sig * (1.0 + gate_pre * (1.0 - sig))).astype(jnp.bfloat16)
        up_grad = (hidden_grad * lift).astype(jnp.bfloat16)
        grad_down = jnp.dot(act.T, sent, preferred_element_type=jnp.float32).astype(jnp.bfloat16)
        slot_grad = (jnp.dot(gate_grad, w_gate[expert].T, preferred_element_type=jnp.float32)
                     + jnp.dot(up_grad, w_up[expert].T, preferred_element_type=jnp.float32)).astype(jnp.bfloat16)
        return grad_down, slot_grad

    grad_down, slot_grad = lax.map(per_expert, jnp.arange(EXPERTS, dtype=jnp.int32))
    clipped = jnp.where(in_window, route_ids, 0).astype(jnp.int32)
    ids_grouped = clipped.reshape(N_DP, TOKENS // N_DP, TOPK)
    pos_grouped = slot_pos.reshape(N_DP, TOKENS // N_DP, TOPK)
    keep_grouped = in_window.reshape(N_DP, TOKENS // N_DP, TOPK)

    def combine(triple):
        ids_block, pos_block, keep_block = triple
        rows = slot_grad[ids_block, pos_block].astype(jnp.float32)
        rows = jnp.where(keep_block[:, :, None], rows, jnp.float32(0.0))
        return jnp.sum(rows, axis=1).astype(jnp.bfloat16)

    input_grad = lax.map(combine, (ids_grouped, pos_grouped, keep_grouped)).reshape(TOKENS, D)
    return input_grad, grad_down
```

```python
import jax
import jax.numpy as jnp
from jax import lax
from jax.experimental import pallas as pl
from jax.experimental.pallas import tpu as pltpu
from jax.sharding import Mesh, PartitionSpec as P

BF = jnp.bfloat16
F32 = jnp.float32

N_EXP = 32
CAP = 5
TOK = 128
GX = 4
GY = 4
WIDE = 1280
HALF = 640
PIECE = 256
HID = 768
LEAD = 4
ROWS_A = N_EXP * LEAD
ROWS_B = N_EXP
VMEM_LIMIT = 40 * 1024 * 1024


def iota(shape, dim):
    return lax.broadcasted_iota(jnp.int32, shape, dim)


def nn(left, right):
    return lax.dot_general(left, right, (((1,), (0,)), ((), ())), preferred_element_type=F32)


def nt(left, right):
    return lax.dot_general(left, right, (((1,), (1,)), ((), ())), preferred_element_type=F32)


def tn(left, right):
    return lax.dot_general(left, right, (((0,), (0,)), ((), ())), preferred_element_type=F32)


def one_hot(mask):
    return jnp.where(mask, 1.0, 0.0).astype(BF)


def call(body, out_shape, flops=0, moved=0, **kwargs):
    return pl.pallas_call(
        body,
        out_shape=out_shape,
        compiler_params=pltpu.CompilerParams(vmem_limit_bytes=VMEM_LIMIT),
        cost_estimate=pl.CostEstimate(flops=flops, bytes_accessed=moved, transcendentals=0),
        **kwargs,
    )


def arr(*dims, dtype=BF):
    return jax.ShapeDtypeStruct(dims, dtype)


def match_rows(code, probs, row_code):
    hits = jnp.zeros((256, TOK), F32)
    weight = jnp.zeros((256, TOK), F32)
    for k in range(code.shape[0]):
        same = row_code == code[k : k + 1, :]
        hits = hits + jnp.where(same, 1.0, 0.0)
        if probs is not None:
            weight = weight + jnp.where(same, probs[k : k + 1, :], 0.0)
    return hits, jnp.sum(weight, axis=1, keepdims=True)


def select_a(ids_ref, slots_ref, probs):
    code = ids_ref[...] * CAP + slots_ref[...]
    row = iota((256, TOK), 0)
    hits, weight = match_rows(code, probs, (row // 8) * CAP + row % 4)
    lower = (row % 8) < 4
    return (
        jnp.concatenate([jnp.where(lower, hits, 0.0), jnp.where(lower, 0.0, hits)], axis=1).astype(BF),
        weight,
    )


def select_b(ids_ref, slots_ref, probs):
    code = ids_ref[...] * CAP + slots_ref[...]
    row = iota((256, TOK), 0)
    hits, weight = match_rows(code, probs, (row // 8) * CAP + LEAD)
    return (
        jnp.concatenate([jnp.where(row % 8 == j, hits, 0.0) for j in range(5)], axis=1).astype(BF),
        weight,
    )


def spread_a():
    row = iota((256, 256), 0)
    col = iota((256, 256), 1)
    return one_hot(col == ((row % 128) // 4) * 8 + (row // 128) * 4 + row % 4)


def collect_a():
    row = iota((256, 256), 0)
    col = iota((256, 256), 1)
    return one_hot(row == ((col % 128) // 4) * 8 + (col // 128) * 4 + col % 4)


def spread_b():
    row = iota((160, 256), 0)
    col = iota((160, 256), 1)
    return one_hot(col == (row % 32) * 8 + row // 32)


def collect_b():
    row = iota((256, 160), 0)
    col = iota((256, 160), 1)
    return one_hot(row == (col % 32) * 8 + col // 32)


def pick_kernel(og_ref, ids_ref, slots_ref, probs_ref, msg_ref):
    pick, weight = select_a(ids_ref, slots_ref, probs_ref[...])
    for g in range(GX):
        at = g * WIDE
        both = jnp.concatenate([og_ref[:, at : at + HALF], og_ref[:, at + HALF : at + WIDE]], axis=0)
        rows = nn(pick, both) * weight
        msg_ref[g * N_EXP : (g + 1) * N_EXP] = rows.reshape(N_EXP, 8, HALF).astype(BF)


def pick_last_kernel(og_ref, ids_ref, slots_ref, probs_ref, after_ref, msg_ref):
    pick, weight = select_b(ids_ref, slots_ref, probs_ref[...])
    for g in range(GX):
        at = g * WIDE
        pieces = jnp.concatenate(
            [og_ref[:, at + j * PIECE : at + (j + 1) * PIECE] for j in range(5)], axis=0
        )
        rows = nn(pick, pieces) * weight
        msg_ref[g * N_EXP : (g + 1) * N_EXP] = rows.reshape(N_EXP, 8, PIECE).astype(BF)


def order_kernel(pre_ref, out_ref):
    row = iota((160, 160), 0)
    col = iota((160, 160), 1)
    lead = (row // 4) * CAP + row % 4
    last = (row - ROWS_A) * CAP + LEAD
    moved = nn(one_hot(col == jnp.where(row < ROWS_A, lead, last)), pre_ref[...]).astype(BF)
    for g in range(GX):
        out_ref[g] = moved


def hidden_a_kernel(recv_ref, down_ref, sent_ref, part_ref):
    spread = spread_a()
    for g in range(GX):
        rows = recv_ref[g * N_EXP : (g + 1) * N_EXP].astype(F32).reshape(256, HALF).astype(BF)
        halves = nn(spread, rows).astype(BF)
        sent_ref[g * ROWS_A : (g + 1) * ROWS_A, :HALF] = halves[:ROWS_A]
        sent_ref[g * ROWS_A : (g + 1) * ROWS_A, HALF:] = halves[ROWS_A:]
    for g in range(GX):
        part_ref[g] = nn(sent_ref[g * ROWS_A : (g + 1) * ROWS_A, :], down_ref[...]).astype(BF)


def hidden_b_kernel(recv_ref, down_ref, sent_ref, part_ref):
    spread = spread_b()
    for g in range(GX):
        rows = recv_ref[g * N_EXP : (g + 1) * N_EXP].astype(F32).reshape(256, PIECE).astype(BF)
        pieces = nn(spread, rows).astype(BF)
        for j in range(5):
            sent_ref[g * ROWS_B : (g + 1) * ROWS_B, j * PIECE : (j + 1) * PIECE] = pieces[
                j * ROWS_B : (j + 1) * ROWS_B
            ]
    part = nn(sent_ref[...], down_ref[...]).astype(BF)
    for g in range(GX):
        part_ref[g] = part[g * ROWS_B : (g + 1) * ROWS_B]


def total_kernel(part_ref, out_ref):
    total = part_ref[0].astype(F32)
    for g in range(1, GX):
        total = total + part_ref[g].astype(F32)
    total = total.astype(BF)
    for g in range(GX):
        out_ref[g] = total


def unit_grads(hidden_grad, pre):
    gate_pre = pre[:, :HID].astype(F32)
    up_pre = pre[:, HID:].astype(F32)
    sig = jax.nn.sigmoid(gate_pre)
    gate_grad = (hidden_grad * up_pre * sig * (1.0 + gate_pre * (1.0 - sig))).astype(BF)
    up_grad = (hidden_grad * (gate_pre * sig)).astype(BF)
    return jnp.concatenate([gate_grad, up_grad], axis=1)


def back_a_kernel(hidden_ref, pre_ref, in_ref, msg_ref):
    collect = collect_a()
    for g in range(GX):
        grads = unit_grads(hidden_ref[g].astype(F32), pre_ref[g, :ROWS_A, :])
        rows = nt(grads, in_ref[...]).astype(BF)
        both = jnp.concatenate([rows[:, :HALF], rows[:, HALF:]], axis=0)
        msg_ref[g * N_EXP : (g + 1) * N_EXP] = nn(collect, both).reshape(N_EXP, 8, HALF).astype(BF)


def back_b_kernel(hidden_ref, pre_ref, in_ref, msg_ref):
    collect = collect_b()
    hidden = jnp.concatenate([hidden_ref[g] for g in range(GX)], axis=0).astype(F32)
    pre = jnp.concatenate([pre_ref[g, ROWS_A:, :] for g in range(GX)], axis=0)
    rows = nt(unit_grads(hidden, pre), in_ref[...]).astype(BF)
    for g in range(GX):
        own = rows[g * ROWS_B : (g + 1) * ROWS_B]
        pieces = jnp.concatenate([own[:, j * PIECE : (j + 1) * PIECE] for j in range(5)], axis=0)
        msg_ref[g * N_EXP : (g + 1) * N_EXP] = nn(collect, pieces).reshape(N_EXP, 8, PIECE).astype(BF)


def down_kernel(sent_a_ref, sent_b_ref, pre_ref, out_ref):
    def act_of(pre):
        gate_pre = pre[:, :HID].astype(F32)
        return (gate_pre * jax.nn.sigmoid(gate_pre) * pre[:, HID:].astype(F32)).astype(BF)

    act = jnp.concatenate(
        [act_of(pre_ref[g, :ROWS_A, :]) for g in range(GX)]
        + [act_of(pre_ref[g, ROWS_A:, :]) for g in range(GX)],
        axis=0,
    )
    for j in range(GY):
        at = j * 320
        sent = jnp.concatenate([sent_a_ref[...], sent_b_ref[...]], axis=0)
        if j == 0:
            full = tn(sent, act)
        out_ref[j] = full[at : at + 320].astype(BF)


def down_total_kernel(part_ref, out_ref):
    total = part_ref[0].astype(F32)
    for g in range(1, GY):
        total = total + part_ref[g].astype(F32)
    out_ref[...] = total.astype(BF)


def gather_kernel(ret_a_ref, ret_b_ref, ids_ref, slots_ref, out_ref):
    pick_a, _ = select_a(ids_ref, slots_ref, None)
    pick_b, _ = select_b(ids_ref, slots_ref, None)
    for g in range(GX):
        rows_a = ret_a_ref[g * N_EXP : (g + 1) * N_EXP].astype(F32).reshape(256, HALF).astype(BF)
        rows_b = ret_b_ref[g * N_EXP : (g + 1) * N_EXP].astype(F32).reshape(256, PIECE).astype(BF)
        halves = tn(pick_a, rows_a)
        pieces = tn(pick_b, rows_b)
        lead = jnp.concatenate([halves[:TOK], halves[TOK:]], axis=1)
        last = jnp.concatenate([pieces[j * TOK : (j + 1) * TOK] for j in range(5)], axis=1)
        out_ref[:, g * WIDE : (g + 1) * WIDE] = (lead + last).astype(BF)


def swap(value, axes):
    return lax.all_to_all(value, axes, 0, 0, tiled=True)


def per_device(out_grad, route_ids, route_slots, route_probs, saved_pre, w_gate, w_up, w_down):
    ids, slots, probs = route_ids.T, route_slots.T, route_probs.T
    peers = ("gx", "expert")
    down_w = lax.all_gather(w_down[0].T, "gy", axis=0, tiled=True)
    in_w = lax.all_gather(jnp.concatenate([w_gate[0], w_up[0]], axis=1), "gy", axis=0, tiled=True)

    msg_a = call(pick_kernel, arr(GX * N_EXP, 8, HALF), 1 << 29, 1 << 22)(out_grad, ids, slots, probs)
    recv_a = swap(msg_a, peers)
    pre = swap(call(order_kernel, arr(GX, 160, 2 * HID), 1 << 27, 1 << 21)(saved_pre[0]), "gx")

    sent_a, part_a = call(
        hidden_a_kernel, (arr(GX * ROWS_A, WIDE), arr(GX, ROWS_A, HID)), 1 << 30, 1 << 22
    )(recv_a, down_w)
    msg_b = call(
        pick_last_kernel,
        arr(GX * N_EXP, 8, PIECE),
        1 << 29,
        1 << 21,
        in_specs=[pl.BlockSpec(memory_space=pltpu.VMEM)] * 4 + [pl.BlockSpec(memory_space=pl.ANY)],
    )(out_grad, ids, slots, probs, recv_a)
    recv_b = swap(msg_b, peers)
    hidden_a = swap(call(total_kernel, arr(GX, ROWS_A, HID), 0, 1 << 21)(swap(part_a, "gx")), "gx")
    back_a = swap(
        call(back_a_kernel, arr(GX * N_EXP, 8, HALF), 1 << 31, 1 << 23)(hidden_a, pre, in_w), peers
    )

    sent_b, part_b = call(
        hidden_b_kernel, (arr(GX * ROWS_B, WIDE), arr(GX, ROWS_B, HID)), 1 << 28, 1 << 22
    )(recv_b, down_w)
    hidden_b = swap(call(total_kernel, arr(GX, ROWS_B, HID), 0, 1 << 19)(swap(part_b, "gx")), "gx")
    back_b = swap(
        call(back_b_kernel, arr(GX * N_EXP, 8, PIECE), 1 << 29, 1 << 23)(hidden_b, pre, in_w), peers
    )

    down_part = call(down_kernel, arr(GY, 320, HID), 1 << 30, 1 << 23)(sent_a, sent_b, pre)
    grad_down = call(down_total_kernel, arr(320, HID), 0, 1 << 21)(swap(down_part, "gy"))
    input_grad = call(gather_kernel, arr(TOK, GX * WIDE), 1 << 30, 1 << 22)(back_a, back_b, ids, slots)
    return (input_grad, grad_down.T[None])


def solution(mesh):
    devices = mesh.devices
    grid = Mesh(devices.reshape((GX, GY) + devices.shape[1:]), ("gx", "gy", "expert"))
    rows = P(("gx", "gy", "expert"), None)
    return jax.shard_map(
        per_device,
        mesh=grid,
        in_specs=(
            rows,
            rows,
            rows,
            rows,
            P("expert", ("gx", "gy"), None),
            P("expert", ("gx", "gy"), None),
            P("expert", ("gx", "gy"), None),
            P("expert", None, ("gx", "gy")),
        ),
        out_specs=(rows, P("expert", None, ("gx", "gy"))),
        check_vma=False,
    )
```

```python
import jax
import jax.numpy as jnp
from jax import lax
from jax.experimental import pallas as pl
from jax.experimental.pallas import tpu as pltpu
from jax.sharding import Mesh, PartitionSpec as P

BF = jnp.bfloat16
F32 = jnp.float32

N_EXP = 32
CAP = 5
TOK = 128
GX = 4
GY = 4
WIDE = 1280
HALF = 640
HID = 768
ROWS = N_EXP * CAP
PAIRS = 2 * N_EXP
VMEM_LIMIT = 40 * 1024 * 1024


def iota(shape, dim):
    return lax.broadcasted_iota(jnp.int32, shape, dim)


def nn(left, right):
    return lax.dot_general(left, right, (((1,), (0,)), ((), ())), preferred_element_type=F32)


def nt(left, right):
    return lax.dot_general(left, right, (((1,), (1,)), ((), ())), preferred_element_type=F32)


def tn(left, right):
    return lax.dot_general(left, right, (((0,), (0,)), ((), ())), preferred_element_type=F32)


def one_hot(mask):
    return jnp.where(mask, 1.0, 0.0).astype(BF)


def call(body, out_shape, flops=0, moved=0, **kwargs):
    return pl.pallas_call(
        body,
        out_shape=out_shape,
        compiler_params=pltpu.CompilerParams(vmem_limit_bytes=VMEM_LIMIT),
        cost_estimate=pl.CostEstimate(flops=flops, bytes_accessed=moved, transcendentals=0),
        **kwargs,
    )


def arr(*dims, dtype=BF):
    return jax.ShapeDtypeStruct(dims, dtype)


def select(ids_ref, slots_ref, probs):
    code = ids_ref[...] * CAP + slots_ref[...]
    shape = (CAP * PAIRS, TOK)
    row = iota(shape, 0)
    row_code = ((row % PAIRS) // 2) * CAP + row // PAIRS
    hits = jnp.zeros(shape, F32)
    weight = jnp.zeros(shape, F32)
    for k in range(code.shape[0]):
        same = row_code == code[k : k + 1, :]
        hits = hits + jnp.where(same, 1.0, 0.0)
        if probs is not None:
            weight = weight + jnp.where(same, probs[k : k + 1, :], 0.0)
    lower = row % 2 == 0
    pick = jnp.concatenate([jnp.where(lower, hits, 0.0), jnp.where(lower, 0.0, hits)], axis=1)
    return pick.astype(BF), jnp.sum(weight, axis=1, keepdims=True)


def split_halves():
    row = iota((PAIRS, PAIRS), 0)
    col = iota((PAIRS, PAIRS), 1)
    return one_hot(col == (row % N_EXP) * 2 + row // N_EXP)


def join_halves():
    row = iota((PAIRS, PAIRS), 0)
    col = iota((PAIRS, PAIRS), 1)
    return one_hot(row == (col % N_EXP) * 2 + col // N_EXP)


def pick_kernel(og_ref, ids_ref, slots_ref, probs_ref, msg_ref, pick_ref, weight_ref):
    @pl.when(pl.program_id(0) == 0)
    def _():
        pick, weight = select(ids_ref, slots_ref, probs_ref[...])
        pick_ref[...] = pick
        weight_ref[...] = jnp.broadcast_to(weight, weight_ref.shape)

    both = jnp.concatenate([og_ref[:, :HALF], og_ref[:, HALF:]], axis=0)
    rows = nn(pick_ref[...], both)
    for s in range(CAP):
        span = slice(s * PAIRS, (s + 1) * PAIRS)
        own = rows[span] * weight_ref[span, :1]
        msg_ref[:, :, s * HALF : (s + 1) * HALF] = own.reshape(N_EXP, 2, HALF).astype(BF)


def hidden_kernel(at_ref, recv_ref, weights_ref, after_ref, sent_ref, *part_refs):
    split = split_halves()
    for r in range(GX):
        g = lax.rem(at_ref[0] + (GX - r), GX)
        for s in range(CAP):
            rows = recv_ref[pl.ds(g * N_EXP, N_EXP), :, s * HALF : (s + 1) * HALF]
            rows = rows.astype(F32).reshape(PAIRS, HALF).astype(BF)
            halves = nn(split, rows).astype(BF)
            at = r * ROWS + s * N_EXP
            sent_ref[at : at + N_EXP, :HALF] = halves[:N_EXP]
            sent_ref[at : at + N_EXP, HALF:] = halves[N_EXP:]
    for r in range(GX):
        part_refs[r][...] = nn(sent_ref[r * ROWS : (r + 1) * ROWS, :], weights_ref[:, :HID]).astype(BF)


def back_kernel(at_ref, hidden_0, hidden_1, hidden_2, hidden_3, gate_ref, up_ref, weights_ref, msg_ref):
    join = join_halves()
    grads = []
    for r, hidden_ref in enumerate((hidden_0, hidden_1, hidden_2, hidden_3)):
        hidden = hidden_ref[...].astype(F32)
        span = slice(r * ROWS, (r + 1) * ROWS)
        gate_grad = (hidden * gate_ref[span, :].astype(F32)).astype(BF)
        up_grad = (hidden * up_ref[span, :].astype(F32)).astype(BF)
        grads.append(jnp.concatenate([gate_grad, up_grad], axis=1))
    rows = nt(jnp.concatenate(grads, axis=0), weights_ref[:, HID:]).astype(BF)
    for r in range(GX):
        g = lax.rem(at_ref[0] + (GX - r), GX)
        for s in range(CAP):
            own = rows[r * ROWS + s * N_EXP : r * ROWS + (s + 1) * N_EXP]
            both = jnp.concatenate([own[:, :HALF], own[:, HALF:]], axis=0)
            msg_ref[pl.ds(g * N_EXP, N_EXP), :, s * HALF : (s + 1) * HALF] = (
                nn(join, both).reshape(N_EXP, 2, HALF).astype(BF)
            )


def gather_kernel(ret_ref, ids_ref, slots_ref, out_ref):
    pick, _ = select(ids_ref, slots_ref, None)
    for g in range(GX):
        rows = jnp.concatenate(
            [
                ret_ref[g * N_EXP : (g + 1) * N_EXP, :, s * HALF : (s + 1) * HALF]
                .astype(F32)
                .reshape(PAIRS, HALF)
                .astype(BF)
                for s in range(CAP)
            ],
            axis=0,
        )
        halves = tn(pick, rows).astype(BF)
        out_ref[:, g * WIDE : g * WIDE + HALF] = halves[:TOK]
        out_ref[:, g * WIDE + HALF : (g + 1) * WIDE] = halves[TOK:]


def pack_kernel(down_ref, gate_ref, up_ref, after_ref, out_ref):
    out_ref[:, :HID] = down_ref[...]
    out_ref[:, HID : 2 * HID] = gate_ref[...]
    out_ref[:, 2 * HID :] = up_ref[...]


def order_kernel(pre_ref, after_ref, out_ref):
    row = iota((ROWS, ROWS), 0)
    col = iota((ROWS, ROWS), 1)
    swap_rows = one_hot(col == (row % N_EXP) * CAP + row // N_EXP)
    out_ref[...] = nn(swap_rows, pre_ref[...]).astype(BF)


def factor_kernel(pre_0, pre_1, pre_2, pre_3, gate_ref, up_ref, act_ref):
    for r, pre_ref in enumerate((pre_0, pre_1, pre_2, pre_3)):
        for s in range(CAP):
            span = slice(s * N_EXP, (s + 1) * N_EXP)
            to = slice(r * ROWS + s * N_EXP, r * ROWS + (s + 1) * N_EXP)
            gate_pre = pre_ref[span, :HID].astype(F32)
            up_pre = pre_ref[span, HID:].astype(F32)
            sig = jax.nn.sigmoid(gate_pre)
            lift = gate_pre * sig
            gate_ref[to, :] = (up_pre * sig * (1.0 + gate_pre * (1.0 - sig))).astype(BF)
            up_ref[to, :] = lift.astype(BF)
            act_ref[to, :] = (lift * up_pre).astype(BF)


def total_kernel(part_0, part_1, part_2, part_3, out_ref):
    total = part_0[...].astype(F32) + part_1[...].astype(F32)
    out_ref[...] = (total + (part_2[...].astype(F32) + part_3[...].astype(F32))).astype(BF)


def down_kernel(sent_ref, act_ref, after_ref, out_ref):
    out_ref[...] = tn(sent_ref[...], act_ref[...]).astype(BF)


def swap(value):
    return lax.all_to_all(value, ("gx", "expert"), 0, 0, tiled=True)


def step(value, r):
    return lax.ppermute(value, "gx", [(i, (i + r) % GX) for i in range(GX)])


def per_device(out_grad, route_ids, route_slots, route_probs, saved_pre, w_gate, w_up, w_down):
    ids, slots, probs = route_ids.T, route_slots.T, route_probs.T
    at = lax.axis_index("gx").reshape(1)
    smem = pl.BlockSpec(memory_space=pltpu.SMEM)
    vmem = pl.BlockSpec(memory_space=pltpu.VMEM)

    anywhere = pl.BlockSpec(memory_space=pl.ANY)

    msg = call(
        pick_kernel,
        arr(GX * N_EXP, 2, CAP * HALF),
        1 << 29,
        1 << 22,
        grid=(GX,),
        in_specs=[pl.BlockSpec((TOK, WIDE), lambda g: (0, g))]
        + [pl.BlockSpec(ids.shape, lambda g: (0, 0))] * 3,
        out_specs=pl.BlockSpec((N_EXP, 2, CAP * HALF), lambda g: (g, 0, 0)),
        scratch_shapes=[pltpu.VMEM((CAP * PAIRS, 2 * TOK), BF), pltpu.VMEM((CAP * PAIRS, 128), F32)],
    )(out_grad, ids, slots, probs)
    recv = swap(msg)
    packed = call(
        pack_kernel, arr(320, 3 * HID), 0, 1 << 22, in_specs=[vmem] * 3 + [anywhere]
    )(w_down[0].T, w_gate[0], w_up[0], msg)
    weights = lax.all_gather(packed, "gy", axis=0, tiled=True)
    pre = call(order_kernel, arr(ROWS, 2 * HID), 1 << 27, 1 << 21, in_specs=[vmem, anywhere])(
        saved_pre[0], msg
    )
    gate_of, up_of, act = call(factor_kernel, (arr(GX * ROWS, HID),) * 3, 1 << 25, 1 << 23)(
        pre, *[step(pre, r) for r in range(1, GX)]
    )

    sent, *parts = call(
        hidden_kernel,
        (arr(GX * ROWS, WIDE),) + (arr(ROWS, HID),) * GX,
        1 << 31,
        1 << 23,
        in_specs=[smem, vmem, vmem, anywhere],
    )(at, recv, weights, act)
    hidden = call(total_kernel, arr(ROWS, HID), 0, 1 << 20)(
        parts[0], *[step(parts[GX - r], r) for r in range(1, GX)]
    )
    back = call(
        back_kernel,
        arr(GX * N_EXP, 2, CAP * HALF),
        1 << 32,
        1 << 23,
        in_specs=[smem] + [vmem] * 7,
    )(at, hidden, *[step(hidden, r) for r in range(1, GX)], gate_of, up_of, weights)
    ret = swap(back)

    down = call(
        down_kernel, arr(WIDE, HID), 1 << 31, 1 << 22, in_specs=[vmem, vmem, anywhere]
    )(sent, act, back)
    grad_down = lax.psum_scatter(down, "gy", scatter_dimension=0, tiled=True)
    input_grad = call(gather_kernel, arr(TOK, GX * WIDE), 1 << 30, 1 << 22)(ret, ids, slots)
    return (input_grad, grad_down.T[None])


def solution(mesh):
    devices = mesh.devices
    grid = Mesh(devices.reshape((GX, GY) + devices.shape[1:]), ("gx", "gy", "expert"))
    rows = P(("gx", "gy", "expert"), None)
    return jax.shard_map(
        per_device,
        mesh=grid,
        in_specs=(
            rows,
            rows,
            rows,
            rows,
            P("expert", ("gx", "gy"), None),
            P("expert", ("gx", "gy"), None),
            P("expert", ("gx", "gy"), None),
            P("expert", None, ("gx", "gy")),
        ),
        out_specs=(rows, P("expert", None, ("gx", "gy"))),
        check_vma=False,
    )
```

```python
import jax
import jax.numpy as jnp
from jax import lax
from jax.experimental import pallas as pl
from jax.experimental.pallas import tpu as pltpu
from jax.sharding import Mesh, PartitionSpec as P

BF = jnp.bfloat16
F32 = jnp.float32

N_EXP = 32
CAP = 5
TOK = 128
GX = 4
GY = 4
WIDE = 1280
HALF = 640
HID = 768
ROWS = N_EXP * CAP
PAIRS = 2 * N_EXP
VMEM_LIMIT = 20 * 1024 * 1024
VMEM_MOST = 60 * 1024 * 1024


def iota(shape, dim):
    return lax.broadcasted_iota(jnp.int32, shape, dim)


def nn(left, right):
    return lax.dot_general(left, right, (((1,), (0,)), ((), ())), preferred_element_type=F32)


def nt(left, right):
    return lax.dot_general(left, right, (((1,), (1,)), ((), ())), preferred_element_type=F32)


def tn(left, right):
    return lax.dot_general(left, right, (((0,), (0,)), ((), ())), preferred_element_type=F32)


def one_hot(mask):
    return jnp.where(mask, 1.0, 0.0).astype(BF)


def call(body, out_shape, flops=0, moved=0, limit=VMEM_LIMIT, **kwargs):
    return pl.pallas_call(
        body,
        out_shape=out_shape,
        compiler_params=pltpu.CompilerParams(vmem_limit_bytes=limit),
        cost_estimate=pl.CostEstimate(flops=flops, bytes_accessed=moved, transcendentals=0),
        **kwargs,
    )


def arr(*dims, dtype=BF):
    return jax.ShapeDtypeStruct(dims, dtype)


def select(ids_ref, slots_ref, probs):
    code = ids_ref[...] * CAP + slots_ref[...]
    shape = (CAP * PAIRS, TOK)
    row = iota(shape, 0)
    row_code = ((row % PAIRS) // 2) * CAP + row // PAIRS
    hits = jnp.zeros(shape, F32)
    weight = jnp.zeros(shape, F32)
    for k in range(code.shape[0]):
        same = row_code == code[k : k + 1, :]
        hits = hits + jnp.where(same, 1.0, 0.0)
        if probs is not None:
            weight = weight + jnp.where(same, probs[k : k + 1, :], 0.0)
    lower = row % 2 == 0
    pick = jnp.concatenate([jnp.where(lower, hits, 0.0), jnp.where(lower, 0.0, hits)], axis=1)
    return pick.astype(BF), jnp.sum(weight, axis=1, keepdims=True)


def split_halves():
    row = iota((PAIRS, PAIRS), 0)
    col = iota((PAIRS, PAIRS), 1)
    return one_hot(col == (row % N_EXP) * 2 + row // N_EXP)


def join_halves():
    row = iota((PAIRS, PAIRS), 0)
    col = iota((PAIRS, PAIRS), 1)
    return one_hot(row == (col % N_EXP) * 2 + col // N_EXP)


def pick_kernel(
    og_any, ids_any, slots_any, probs_any, down_any, gate_any, up_any,
    msg_any, packed_any,
    og_ref, ids_ref, slots_ref, probs_ref, msg_ref, og_sem, in_sem, out_sem, pack_sem,
):
    small = [
        pltpu.make_async_copy(src, dst, in_sem.at[i])
        for i, (src, dst) in enumerate(((ids_any, ids_ref), (slots_any, slots_ref), (probs_any, probs_ref)))
    ]
    wide = [
        pltpu.make_async_copy(og_any.at[:, pl.ds(g * WIDE, WIDE)], og_ref.at[g], og_sem.at[g])
        for g in range(GX)
    ]
    packs = [
        pltpu.make_async_copy(src, packed_any.at[:, pl.ds(i * HID, HID)], pack_sem.at[i])
        for i, src in enumerate((down_any, gate_any, up_any))
    ]
    for copy in small + wide + packs:
        copy.start()
    for copy in small:
        copy.wait()
    pick, weight = select(ids_ref, slots_ref, probs_ref[...])
    outs = []
    for g in range(GX):
        wide[g].wait()
        both = jnp.concatenate([og_ref[g, :, :HALF], og_ref[g, :, HALF:]], axis=0)
        rows = nn(pick, both) * weight
        for s in range(CAP):
            own = rows[s * PAIRS : (s + 1) * PAIRS].reshape(N_EXP, 2, HALF).astype(BF)
            msg_ref[g * N_EXP : (g + 1) * N_EXP, :, s * HALF : (s + 1) * HALF] = own
        span = pl.ds(g * N_EXP, N_EXP)
        outs.append(pltpu.make_async_copy(msg_ref.at[span], msg_any.at[span], out_sem.at[g]))
        outs[-1].start()
    for copy in outs + packs:
        copy.wait()


def arrange_kernel(at_ref, own_ref, less_ref, more_ref, far_low_ref, far_high_ref, down_ref, in_ref):
    def put(ref, away, start):
        rows = ref.shape[0]
        q = lax.rem(at_ref[1] + away, GY)
        to = pl.ds(pl.multiple_of(q * 320 + start, 32), rows)
        down_ref[to, :] = ref[:, :HID]
        in_ref[to, :] = ref[:, HID:]

    put(own_ref, 0, 0)
    put(less_ref, GY - 1, 0)
    put(more_ref, 1, 0)
    put(far_low_ref, 2, 0)
    put(far_high_ref, 2, 160)


def hidden_kernel(at_ref, recv_ref, down_any, after_ref, sent_ref, part_ref, down_ref, sem):
    fetch = pltpu.make_async_copy(down_any, down_ref, sem)
    fetch.start()
    split = split_halves()
    for r in range(GX):
        g = lax.rem(at_ref[0] + (GX - r), GX)
        for s in range(CAP):
            rows = recv_ref[pl.ds(g * N_EXP, N_EXP), :, s * HALF : (s + 1) * HALF]
            rows = rows.astype(F32).reshape(PAIRS, HALF).astype(BF)
            halves = nn(split, rows).astype(BF)
            at = r * ROWS + s * N_EXP
            sent_ref[at : at + N_EXP, :HALF] = halves[:N_EXP]
            sent_ref[at : at + N_EXP, HALF:] = halves[N_EXP:]
    fetch.wait()
    for r in range(GX):
        g = lax.rem(at_ref[0] + (GX - r), GX)
        part_ref[g] = nn(sent_ref[r * ROWS : (r + 1) * ROWS, :], down_ref[...]).astype(BF)


def back_kernel(at_ref, hidden_ref, gate_ref, up_ref, in_ref, msg_ref):
    join = join_halves()
    grads = []
    for r in range(GX):
        hidden = hidden_ref[lax.rem(at_ref[0] + (GX - r), GX)].astype(F32)
        span = slice(r * ROWS, (r + 1) * ROWS)
        gate_grad = (hidden * gate_ref[span, :].astype(F32)).astype(BF)
        up_grad = (hidden * up_ref[span, :].astype(F32)).astype(BF)
        grads.append(jnp.concatenate([gate_grad, up_grad], axis=1))
    rows = nt(jnp.concatenate(grads, axis=0), in_ref[...]).astype(BF)
    for r in range(GX):
        g = lax.rem(at_ref[0] + (GX - r), GX)
        for s in range(CAP):
            own = rows[r * ROWS + s * N_EXP : r * ROWS + (s + 1) * N_EXP]
            both = jnp.concatenate([own[:, :HALF], own[:, HALF:]], axis=0)
            msg_ref[pl.ds(g * N_EXP, N_EXP), :, s * HALF : (s + 1) * HALF] = (
                nn(join, both).reshape(N_EXP, 2, HALF).astype(BF)
            )


def gather_kernel(ret_ref, ids_ref, slots_ref, out_ref):
    pick, _ = select(ids_ref, slots_ref, None)
    for g in range(GX):
        rows = jnp.concatenate(
            [
                ret_ref[g * N_EXP : (g + 1) * N_EXP, :, s * HALF : (s + 1) * HALF]
                .astype(F32)
                .reshape(PAIRS, HALF)
                .astype(BF)
                for s in range(CAP)
            ],
            axis=0,
        )
        halves = tn(pick, rows).astype(BF)
        out_ref[:, g * WIDE : g * WIDE + HALF] = halves[:TOK]
        out_ref[:, g * WIDE + HALF : (g + 1) * WIDE] = halves[TOK:]


def order_kernel(pre_ref, after_ref, out_ref):
    row = iota((ROWS, ROWS), 0)
    col = iota((ROWS, ROWS), 1)
    swap_rows = one_hot(col == (row % N_EXP) * CAP + row // N_EXP)
    out_ref[...] = nn(swap_rows, pre_ref[...]).astype(BF)


def factor_kernel(pre_0, pre_1, pre_2, pre_3, gate_ref, up_ref, act_ref):
    for r, pre_ref in enumerate((pre_0, pre_1, pre_2, pre_3)):
        for s in range(CAP):
            span = slice(s * N_EXP, (s + 1) * N_EXP)
            to = slice(r * ROWS + s * N_EXP, r * ROWS + (s + 1) * N_EXP)
            gate_pre = pre_ref[span, :HID].astype(F32)
            up_pre = pre_ref[span, HID:].astype(F32)
            sig = jax.nn.sigmoid(gate_pre)
            lift = gate_pre * sig
            gate_ref[to, :] = (up_pre * sig * (1.0 + gate_pre * (1.0 - sig))).astype(BF)
            up_ref[to, :] = lift.astype(BF)
            act_ref[to, :] = (lift * up_pre).astype(BF)


def total_kernel(part_ref, out_ref):
    total = (part_ref[0].astype(F32) + part_ref[1].astype(F32)) + (
        part_ref[2].astype(F32) + part_ref[3].astype(F32)
    )
    total = total.astype(BF)
    for g in range(GX):
        out_ref[g] = total


def down_kernel(at_ref, sent_ref, act_ref, after_ref, out_0, out_1, out_2, out_3, full_ref):
    full_ref[...] = tn(sent_ref[...], act_ref[...]).astype(BF)
    for r, out_ref in enumerate((out_0, out_1, out_2, out_3)):
        q = lax.rem(at_ref[1] + r, GY)
        out_ref[...] = full_ref[pl.ds(pl.multiple_of(q * 320, 64), 320), :]


def down_total_kernel(part_0, part_1, part_2, part_3, out_ref):
    total = part_0[...].astype(F32) + part_1[...].astype(F32)
    out_ref[...] = (total + (part_2[...].astype(F32) + part_3[...].astype(F32))).astype(BF)


def swap(value):
    return lax.all_to_all(value, ("gx", "expert"), 0, 0, tiled=True)


def swap_gx(value):
    return lax.all_to_all(value, "gx", 0, 0, tiled=True)


def step(value, axis, r):
    return lax.ppermute(value, axis, [(i, (i + r) % 4) for i in range(4)])


def per_device(out_grad, route_ids, route_slots, route_probs, saved_pre, w_gate, w_up, w_down):
    ids, slots, probs = route_ids.T, route_slots.T, route_probs.T
    at = jnp.stack([lax.axis_index("gx"), lax.axis_index("gy")])
    smem = pl.BlockSpec(memory_space=pltpu.SMEM)
    vmem = pl.BlockSpec(memory_space=pltpu.VMEM)
    anywhere = pl.BlockSpec(memory_space=pl.ANY)

    msg, packed = call(
        pick_kernel,
        (arr(GX * N_EXP, 2, CAP * HALF), arr(320, 3 * HID)),
        1 << 29,
        1 << 23,
        VMEM_MOST,
        in_specs=[anywhere] * 7,
        out_specs=(anywhere, anywhere),
        scratch_shapes=[
            pltpu.VMEM((GX, TOK, WIDE), BF),
            pltpu.VMEM(ids.shape, jnp.int32),
            pltpu.VMEM(ids.shape, jnp.int32),
            pltpu.VMEM(ids.shape, F32),
            pltpu.VMEM((GX * N_EXP, 2, CAP * HALF), BF),
            pltpu.SemaphoreType.DMA((GX,)),
            pltpu.SemaphoreType.DMA((3,)),
            pltpu.SemaphoreType.DMA((GX,)),
            pltpu.SemaphoreType.DMA((3,)),
        ],
    )(out_grad, ids, slots, probs, w_down[0].T, w_gate[0], w_up[0])
    recv = swap(msg)

    less, more = step(packed, "gy", 1), step(packed, "gy", 3)
    far = (step(less[:160], "gy", 1), step(more[160:], "gy", 3))
    down_w, in_w = call(
        arrange_kernel,
        (arr(WIDE, HID), arr(WIDE, 2 * HID)),
        0,
        1 << 24,
        in_specs=[smem] + [vmem] * 5,
    )(at, packed, less, more, *far)
    pre = call(order_kernel, arr(ROWS, 2 * HID), 1 << 27, 1 << 21, in_specs=[vmem, anywhere])(
        saved_pre[0], msg
    )
    gate_of, up_of, act = call(factor_kernel, (arr(GX * ROWS, HID),) * 3, 1 << 25, 1 << 23)(
        pre, *[step(pre, "gx", r) for r in range(1, GX)]
    )

    sent, part = call(
        hidden_kernel,
        (arr(GX * ROWS, WIDE), arr(GX, ROWS, HID)),
        1 << 31,
        1 << 23,
        VMEM_MOST,
        in_specs=[smem, vmem, anywhere, anywhere],
        scratch_shapes=[pltpu.VMEM((WIDE, HID), BF), pltpu.SemaphoreType.DMA],
    )(at, recv, down_w, act)
    hidden = swap_gx(call(total_kernel, arr(GX, ROWS, HID), 0, 1 << 21)(swap_gx(part)))
    back = call(
        back_kernel,
        arr(GX * N_EXP, 2, CAP * HALF),
        1 << 32,
        1 << 23,
        in_specs=[smem] + [vmem] * 4,
    )(at, hidden, gate_of, up_of, in_w)
    ret = swap(back)

    downs = call(
        down_kernel,
        (arr(320, HID),) * GY,
        1 << 31,
        1 << 22,
        in_specs=[smem, vmem, vmem, anywhere],
        scratch_shapes=[pltpu.VMEM((WIDE, HID), BF)],
    )(at, sent, act, back)
    grad_down = call(down_total_kernel, arr(320, HID), 0, 1 << 21)(
        downs[0], *[step(downs[r], "gy", r) for r in range(1, GY)]
    )
    input_grad = call(gather_kernel, arr(TOK, GX * WIDE), 1 << 30, 1 << 22)(ret, ids, slots)
    return (input_grad, grad_down.T[None])


def solution(mesh):
    devices = mesh.devices
    grid = Mesh(devices.reshape((GX, GY) + devices.shape[1:]), ("gx", "gy", "expert"))
    rows = P(("gx", "gy", "expert"), None)
    return jax.shard_map(
        per_device,
        mesh=grid,
        in_specs=(
            rows,
            rows,
            rows,
            rows,
            P("expert", ("gx", "gy"), None),
            P("expert", ("gx", "gy"), None),
            P("expert", ("gx", "gy"), None),
            P("expert", None, ("gx", "gy")),
        ),
        out_specs=(rows, P("expert", None, ("gx", "gy"))),
        check_vma=False,
    )
```

```python
import functools

import jax
import jax.numpy as jnp
from jax import lax
from jax.experimental import pallas as pl
from jax.experimental.pallas import tpu as pltpu
from jax.sharding import Mesh, PartitionSpec as P

BF = jnp.bfloat16
F32 = jnp.float32

N_EXP = 32
CAP = 5
CHUNKS = ((0, 2), (2, 5))
TOK = 128
GX = 4
GY = 4
WIDE = 1280
HALF = 640
HID = 768
ROWS = N_EXP * CAP
PAIRS = 2 * N_EXP
PART = 320
VMEM_LIMIT = 16 * 1024 * 1024
VMEM_MOST = 60 * 1024 * 1024


def iota(shape, dim):
    return lax.broadcasted_iota(jnp.int32, shape, dim)


def nn(left, right):
    return lax.dot_general(left, right, (((1,), (0,)), ((), ())), preferred_element_type=F32)


def nt(left, right):
    return lax.dot_general(left, right, (((1,), (1,)), ((), ())), preferred_element_type=F32)


def tn(left, right):
    return lax.dot_general(left, right, (((0,), (0,)), ((), ())), preferred_element_type=F32)


def one_hot(mask):
    return jnp.where(mask, 1.0, 0.0).astype(BF)


def call(body, out_shape, flops=0, moved=0, limit=VMEM_LIMIT, **kwargs):
    return pl.pallas_call(
        body,
        out_shape=out_shape,
        compiler_params=pltpu.CompilerParams(vmem_limit_bytes=limit),
        cost_estimate=pl.CostEstimate(flops=flops, bytes_accessed=moved, transcendentals=0),
        **kwargs,
    )


def arr(*dims, dtype=BF):
    return jax.ShapeDtypeStruct(dims, dtype)


def select(ids_ref, slots_ref, probs, chunk):
    code = ids_ref[...] * CAP + slots_ref[...]
    shape = ((chunk[1] - chunk[0]) * PAIRS, TOK)
    row = iota(shape, 0)
    row_code = ((row % PAIRS) // 2) * CAP + row // PAIRS + chunk[0]
    hits = jnp.zeros(shape, F32)
    weight = jnp.zeros(shape, F32)
    for k in range(code.shape[0]):
        same = row_code == code[k : k + 1, :]
        hits = hits + jnp.where(same, 1.0, 0.0)
        if probs is not None:
            weight = weight + jnp.where(same, probs[k : k + 1, :], 0.0)
    lower = row % 2 == 0
    pick = jnp.concatenate([jnp.where(lower, hits, 0.0), jnp.where(lower, 0.0, hits)], axis=1)
    return pick.astype(BF), jnp.sum(weight, axis=1, keepdims=True)


def split_halves():
    row = iota((PAIRS, PAIRS), 0)
    col = iota((PAIRS, PAIRS), 1)
    return one_hot(col == (row % N_EXP) * 2 + row // N_EXP)


def join_halves():
    row = iota((PAIRS, PAIRS), 0)
    col = iota((PAIRS, PAIRS), 1)
    return one_hot(row == (col % N_EXP) * 2 + col // N_EXP)


def to_pairs(rows):
    return rows.reshape(N_EXP, 2, HALF).astype(BF)


def from_pairs(block):
    return block.astype(F32).reshape(PAIRS, HALF).astype(BF)


def pick_kernel(chunk, packs, *refs):
    ins, refs = refs[: 4 + max(packs, 1)], refs[4 + max(packs, 1) :]
    outs, refs = refs[: 1 + (packs > 0) * 2], refs[1 + (packs > 0) * 2 :]
    og_any, ids_any, slots_any, probs_any = ins[:4]
    msg_any = outs[0]
    og_ref, ids_ref, slots_ref, probs_ref, msg_ref, og_sem, in_sem, out_sem = refs[:8]
    small = [
        pltpu.make_async_copy(src, dst, in_sem.at[i])
        for i, (src, dst) in enumerate(((ids_any, ids_ref), (slots_any, slots_ref), (probs_any, probs_ref)))
    ]
    wide = [
        pltpu.make_async_copy(og_any.at[:, pl.ds(g * WIDE, WIDE)], og_ref.at[g], og_sem.at[g])
        for g in range(GX)
    ]
    fetches, stores = [], []
    if packs:
        down_any, gate_any, up_any = ins[4:]
        down_ref, in_ref, fetch_sem, store_sem = refs[8:]
        fetches = [
            pltpu.make_async_copy(down_any, down_ref, fetch_sem.at[0]),
            pltpu.make_async_copy(gate_any, in_ref.at[:, pl.ds(0, HID)], fetch_sem.at[1]),
            pltpu.make_async_copy(up_any, in_ref.at[:, pl.ds(HID, HID)], fetch_sem.at[2]),
        ]
        stores = [
            pltpu.make_async_copy(down_ref, outs[1], store_sem.at[0]),
            pltpu.make_async_copy(in_ref, outs[2], store_sem.at[1]),
        ]
    for copy in small + wide + fetches:
        copy.start()
    for copy in small:
        copy.wait()
    pick, weight = select(ids_ref, slots_ref, probs_ref[...], chunk)
    sends = []
    for g in range(GX):
        wide[g].wait()
        both = jnp.concatenate([og_ref[g, :, :HALF], og_ref[g, :, HALF:]], axis=0)
        rows = nn(pick, both) * weight
        for s in range(chunk[1] - chunk[0]):
            msg_ref[g * N_EXP : (g + 1) * N_EXP, :, s * HALF : (s + 1) * HALF] = to_pairs(
                rows[s * PAIRS : (s + 1) * PAIRS]
            )
        span = pl.ds(g * N_EXP, N_EXP)
        sends.append(pltpu.make_async_copy(msg_ref.at[span], msg_any.at[span], out_sem.at[g]))
        sends[-1].start()
        if g == 1:
            for copy in fetches:
                copy.wait()
            for copy in stores:
                copy.start()
    for copy in sends + stores:
        copy.wait()


def arrange_kernel(at_ref, own_ref, piece_1, piece_2, piece_3, out_ref):
    for r, ref in enumerate((own_ref, piece_1, piece_2, piece_3)):
        q = lax.rem(at_ref[1] + (GY - r), GY)
        out_ref[pl.ds(pl.multiple_of(q * PART, 64), PART), :] = ref[...]


def order_kernel(pre_ref, after_ref, out_ref):
    row = iota((ROWS, ROWS), 0)
    col = iota((ROWS, ROWS), 1)
    swap_rows = one_hot(col == (row % N_EXP) * CAP + row // N_EXP)
    out_ref[...] = nn(swap_rows, pre_ref[...]).astype(BF)


def factor_kernel(pre_0, pre_1, pre_2, pre_3, factor_ref, act_ref):
    for r, pre_ref in enumerate((pre_0, pre_1, pre_2, pre_3)):
        for s in range(CAP):
            span = slice(s * N_EXP, (s + 1) * N_EXP)
            gate_pre = pre_ref[span, :HID].astype(F32)
            up_pre = pre_ref[span, HID:].astype(F32)
            sig = jax.nn.sigmoid(gate_pre)
            lift = gate_pre * sig
            factor_ref[r, span, :HID] = (up_pre * sig * (1.0 + gate_pre * (1.0 - sig))).astype(BF)
            factor_ref[r, span, HID:] = lift.astype(BF)
            act_ref[r, span, :] = (lift * up_pre).astype(BF)


def hidden_kernel(n, at_ref, recv_ref, down_ref, sent_ref, *part_refs):
    split = split_halves()
    for r in range(GX):
        g = lax.rem(at_ref[0] + (GX - r), GX)
        for s in range(n):
            rows = from_pairs(recv_ref[pl.ds(g * N_EXP, N_EXP), :, s * HALF : (s + 1) * HALF])
            halves = nn(split, rows).astype(BF)
            span = slice(s * N_EXP, (s + 1) * N_EXP)
            sent_ref[r, span, :HALF] = halves[:N_EXP]
            sent_ref[r, span, HALF:] = halves[N_EXP:]
    for r in range(GX):
        part_refs[r][...] = nn(sent_ref[r], down_ref[...]).astype(BF)


def total_kernel(part_0, part_1, part_2, part_3, out_ref):
    total = part_0[...].astype(F32) + part_1[...].astype(F32)
    out_ref[...] = (total + (part_2[...].astype(F32) + part_3[...].astype(F32))).astype(BF)


def back_kernel(chunk, at_ref, hidden_0, hidden_1, hidden_2, hidden_3, factor_ref, in_ref, msg_ref):
    n = chunk[1] - chunk[0]
    span = slice(chunk[0] * N_EXP, chunk[1] * N_EXP)
    grads = []
    for r, hidden_ref in enumerate((hidden_0, hidden_1, hidden_2, hidden_3)):
        hidden = hidden_ref[...].astype(F32)
        gate_grad = (hidden * factor_ref[r, span, :HID].astype(F32)).astype(BF)
        up_grad = (hidden * factor_ref[r, span, HID:].astype(F32)).astype(BF)
        grads.append(jnp.concatenate([gate_grad, up_grad], axis=1))
    rows = nt(jnp.concatenate(grads, axis=0), in_ref[...]).astype(BF)
    join = join_halves()
    for r in range(GX):
        g = lax.rem(at_ref[0] + (GX - r), GX)
        for s in range(n):
            own = rows[(r * n + s) * N_EXP : (r * n + s + 1) * N_EXP]
            both = jnp.concatenate([own[:, :HALF], own[:, HALF:]], axis=0)
            msg_ref[pl.ds(g * N_EXP, N_EXP), :, s * HALF : (s + 1) * HALF] = to_pairs(nn(join, both))


def down_kernel(at_ref, sent_a_ref, sent_b_ref, act_ref, after_ref, out_0, out_1, out_2, out_3, full_ref):
    sent = jnp.concatenate([ref[r] for r in range(GX) for ref in (sent_a_ref, sent_b_ref)], axis=0)
    act = jnp.concatenate([act_ref[r] for r in range(GX)], axis=0)
    full_ref[...] = tn(sent, act).astype(BF)
    for r, out_ref in enumerate((out_0, out_1, out_2, out_3)):
        q = lax.rem(at_ref[1] + r, GY)
        out_ref[...] = full_ref[pl.ds(pl.multiple_of(q * PART, 64), PART), :]


def gather_kernel(ret_a_ref, ret_b_ref, ids_ref, slots_ref, out_ref):
    picks = [select(ids_ref, slots_ref, None, chunk)[0] for chunk in CHUNKS]
    for g in range(GX):
        halves = 0.0
        for pick, chunk, ret_ref in zip(picks, CHUNKS, (ret_a_ref, ret_b_ref)):
            rows = jnp.concatenate(
                [
                    from_pairs(ret_ref[g * N_EXP : (g + 1) * N_EXP, :, s * HALF : (s + 1) * HALF])
                    for s in range(chunk[1] - chunk[0])
                ],
                axis=0,
            )
            halves = halves + tn(pick, rows)
        halves = halves.astype(BF)
        out_ref[:, g * WIDE : g * WIDE + HALF] = halves[:TOK]
        out_ref[:, g * WIDE + HALF : (g + 1) * WIDE] = halves[TOK:]


def swap(value):
    return lax.all_to_all(value, ("gx", "expert"), 0, 0, tiled=True)


def step(value, axis, r):
    return lax.ppermute(value, axis, [(i, (i + r) % 4) for i in range(4)])


def steps(value, axis):
    return [step(value, axis, r) for r in range(1, 4)]


def per_device(out_grad, route_ids, route_slots, route_probs, saved_pre, w_gate, w_up, w_down):
    ids, slots, probs = route_ids.T, route_slots.T, route_probs.T
    at = jnp.stack([lax.axis_index("gx"), lax.axis_index("gy")])
    smem = pl.BlockSpec(memory_space=pltpu.SMEM)
    vmem = pl.BlockSpec(memory_space=pltpu.VMEM)
    anywhere = pl.BlockSpec(memory_space=pl.ANY)
    size = [(chunk[1] - chunk[0]) for chunk in CHUNKS]
    message = [arr(GX * N_EXP, 2, n * HALF) for n in size]

    def pick(chunk, shapes, operands, packs):
        return call(
            functools.partial(pick_kernel, chunk, packs),
            shapes,
            1 << 29,
            1 << 23,
            VMEM_MOST if packs else VMEM_LIMIT,
            in_specs=[anywhere] * len(operands),
            out_specs=[anywhere] * len(shapes),
            scratch_shapes=[
                pltpu.VMEM((GX, TOK, WIDE), BF),
                pltpu.VMEM(ids.shape, jnp.int32),
                pltpu.VMEM(ids.shape, jnp.int32),
                pltpu.VMEM(ids.shape, F32),
                pltpu.VMEM(shapes[0].shape, BF),
                pltpu.SemaphoreType.DMA((GX,)),
                pltpu.SemaphoreType.DMA((3,)),
                pltpu.SemaphoreType.DMA((GX,)),
            ]
            + [
                pltpu.VMEM((PART, HID), BF),
                pltpu.VMEM((PART, 2 * HID), BF),
                pltpu.SemaphoreType.DMA((3,)),
                pltpu.SemaphoreType.DMA((2,)),
            ]
            * (packs > 0),
        )(*operands)

    routes = (out_grad, ids, slots, probs)
    msg_a, own_down, own_in = pick(
        CHUNKS[0],
        [message[0], arr(PART, HID), arr(PART, 2 * HID)],
        (*routes, w_down[0].T, w_gate[0], w_up[0]),
        3,
    )
    recv_a = swap(msg_a)
    (msg_b,) = pick(CHUNKS[1], [message[1]], (*routes, msg_a), 0)
    recv_b = swap(msg_b)

    def arrange(own):
        return call(
            arrange_kernel,
            arr(WIDE, own.shape[1]),
            0,
            1 << 23,
            in_specs=[smem] + [vmem] * 4,
        )(at, own, *steps(own, "gy"))

    down_w, in_w = arrange(own_down), arrange(own_in)
    pre = call(order_kernel, arr(ROWS, 2 * HID), 1 << 27, 1 << 21, in_specs=[vmem, anywhere])(
        saved_pre[0], msg_a
    )
    factors, act = call(
        factor_kernel, (arr(GX, ROWS, 2 * HID), arr(GX, ROWS, HID)), 1 << 25, 1 << 23
    )(pre, *steps(pre, "gx"))

    def middle(c, recv):
        rows = size[c] * N_EXP
        sent, *parts = call(
            functools.partial(hidden_kernel, size[c]),
            (arr(GX, rows, WIDE),) + (arr(rows, HID),) * GX,
            1 << 30,
            1 << 23,
            in_specs=[smem, vmem, vmem],
        )(at, recv, down_w)
        hidden = call(total_kernel, arr(rows, HID), 0, 1 << 20)(
            parts[0], *[step(parts[GX - r], "gx", r) for r in range(1, GX)]
        )
        back = call(
            functools.partial(back_kernel, CHUNKS[c]),
            message[c],
            1 << 31,
            1 << 23,
            in_specs=[smem] + [vmem] * 6,
        )(at, hidden, *steps(hidden, "gx"), factors, in_w)
        return sent, back

    sent_a, back_a = middle(0, recv_a)
    ret_a = swap(back_a)
    sent_b, back_b = middle(1, recv_b)
    ret_b = swap(back_b)

    downs = call(
        down_kernel,
        (arr(PART, HID),) * GY,
        1 << 31,
        1 << 22,
        in_specs=[smem] + [vmem] * 3 + [anywhere],
        scratch_shapes=[pltpu.VMEM((WIDE, HID), BF)],
    )(at, sent_a, sent_b, act, back_b)
    grad_down = call(total_kernel, arr(PART, HID), 0, 1 << 21)(
        downs[0], *[step(downs[r], "gy", r) for r in range(1, GY)]
    )
    input_grad = call(gather_kernel, arr(TOK, GX * WIDE), 1 << 30, 1 << 22)(ret_a, ret_b, ids, slots)
    return (input_grad, grad_down.T[None])


def solution(mesh):
    devices = mesh.devices
    grid = Mesh(devices.reshape((GX, GY) + devices.shape[1:]), ("gx", "gy", "expert"))
    rows = P(("gx", "gy", "expert"), None)
    return jax.shard_map(
        per_device,
        mesh=grid,
        in_specs=(
            rows,
            rows,
            rows,
            rows,
            P("expert", ("gx", "gy"), None),
            P("expert", ("gx", "gy"), None),
            P("expert", ("gx", "gy"), None),
            P("expert", None, ("gx", "gy")),
        ),
        out_specs=(rows, P("expert", None, ("gx", "gy"))),
        check_vma=False,
    )
```

```python
import jax
import jax.numpy as jnp
from jax import lax
from jax.experimental import pallas as pl
from jax.experimental.pallas import tpu as pltpu
from jax.sharding import Mesh, PartitionSpec as P

BF = jnp.bfloat16
F32 = jnp.float32

N_EXP = 32
CAP = 5
TOK = 128
GX = 4
GY = 4
WIDE = 1280
HALF = 640
HID = 768
ROWS = N_EXP * CAP
PAIRS = 2 * N_EXP
PART = 320
VMEM_LIMIT = 16 * 1024 * 1024
VMEM_MOST = 60 * 1024 * 1024


def iota(shape, dim):
    return lax.broadcasted_iota(jnp.int32, shape, dim)


def nn(left, right):
    return lax.dot_general(left, right, (((1,), (0,)), ((), ())), preferred_element_type=F32)


def nt(left, right):
    return lax.dot_general(left, right, (((1,), (1,)), ((), ())), preferred_element_type=F32)


def tn(left, right):
    return lax.dot_general(left, right, (((0,), (0,)), ((), ())), preferred_element_type=F32)


def one_hot(mask):
    return jnp.where(mask, 1.0, 0.0).astype(BF)


def call(body, out_shape, flops=0, moved=0, limit=VMEM_LIMIT, **kwargs):
    return pl.pallas_call(
        body,
        out_shape=out_shape,
        compiler_params=pltpu.CompilerParams(vmem_limit_bytes=limit),
        cost_estimate=pl.CostEstimate(flops=flops, bytes_accessed=moved, transcendentals=0),
        **kwargs,
    )


def arr(*dims, dtype=BF):
    return jax.ShapeDtypeStruct(dims, dtype)


def select(ids_ref, slots_ref, probs):
    code = ids_ref[...] * CAP + slots_ref[...]
    shape = (CAP * PAIRS, TOK)
    row = iota(shape, 0)
    row_code = ((row % PAIRS) // 2) * CAP + row // PAIRS
    hits = jnp.zeros(shape, F32)
    weight = jnp.zeros(shape, F32)
    for k in range(code.shape[0]):
        same = row_code == code[k : k + 1, :]
        hits = hits + jnp.where(same, 1.0, 0.0)
        if probs is not None:
            weight = weight + jnp.where(same, probs[k : k + 1, :], 0.0)
    lower = row % 2 == 0
    pick = jnp.concatenate([jnp.where(lower, hits, 0.0), jnp.where(lower, 0.0, hits)], axis=1)
    return pick.astype(BF), jnp.sum(weight, axis=1, keepdims=True)


def split_halves():
    row = iota((PAIRS, PAIRS), 0)
    col = iota((PAIRS, PAIRS), 1)
    return one_hot(col == (row % N_EXP) * 2 + row // N_EXP)


def join_halves():
    row = iota((PAIRS, PAIRS), 0)
    col = iota((PAIRS, PAIRS), 1)
    return one_hot(row == (col % N_EXP) * 2 + col // N_EXP)


def to_pairs(rows):
    return rows.reshape(N_EXP, 2, HALF).astype(BF)


def from_pairs(block):
    return block.astype(F32).reshape(PAIRS, HALF).astype(BF)


def pick_kernel(
    og_any, ids_any, slots_any, probs_any, down_any, gate_any, up_any,
    msg_any, own_down_any, own_in_any,
    og_ref, ids_ref, slots_ref, probs_ref, msg_ref, down_ref, in_ref,
    og_sem, in_sem, out_sem, fetch_sem, store_sem,
):
    small = [
        pltpu.make_async_copy(src, dst, in_sem.at[i])
        for i, (src, dst) in enumerate(((ids_any, ids_ref), (slots_any, slots_ref), (probs_any, probs_ref)))
    ]
    wide = [
        pltpu.make_async_copy(og_any.at[:, pl.ds(g * WIDE, WIDE)], og_ref.at[g], og_sem.at[g])
        for g in range(GX)
    ]
    fetches = [
        pltpu.make_async_copy(down_any, down_ref, fetch_sem.at[0]),
        pltpu.make_async_copy(gate_any, in_ref.at[:, pl.ds(0, HID)], fetch_sem.at[1]),
        pltpu.make_async_copy(up_any, in_ref.at[:, pl.ds(HID, HID)], fetch_sem.at[2]),
    ]
    stores = [
        pltpu.make_async_copy(down_ref, own_down_any, store_sem.at[0]),
        pltpu.make_async_copy(in_ref, own_in_any, store_sem.at[1]),
    ]
    for copy in small + wide + fetches:
        copy.start()
    for copy in small:
        copy.wait()
    pick, weight = select(ids_ref, slots_ref, probs_ref[...])
    sends = []
    for g in range(GX):
        wide[g].wait()
        both = jnp.concatenate([og_ref[g, :, :HALF], og_ref[g, :, HALF:]], axis=0)
        rows = nn(pick, both) * weight
        for s in range(CAP):
            msg_ref[g * N_EXP : (g + 1) * N_EXP, :, s * HALF : (s + 1) * HALF] = to_pairs(
                rows[s * PAIRS : (s + 1) * PAIRS]
            )
        span = pl.ds(g * N_EXP, N_EXP)
        sends.append(pltpu.make_async_copy(msg_ref.at[span], msg_any.at[span], out_sem.at[g]))
        sends[-1].start()
        if g == 1:
            for copy in fetches:
                copy.wait()
            for copy in stores:
                copy.start()
    for copy in sends + stores:
        copy.wait()


def arrange_kernel(at_ref, own_ref, piece_1, piece_2, piece_3, out_ref):
    for r, ref in enumerate((own_ref, piece_1, piece_2, piece_3)):
        q = lax.rem(at_ref[1] + (GY - r), GY)
        out_ref[pl.ds(pl.multiple_of(q * PART, 64), PART), :] = ref[...]


def order_kernel(pre_ref, after_ref, out_ref):
    row = iota((ROWS, ROWS), 0)
    col = iota((ROWS, ROWS), 1)
    swap_rows = one_hot(col == (row % N_EXP) * CAP + row // N_EXP)
    out_ref[...] = nn(swap_rows, pre_ref[...]).astype(BF)


def factor_kernel(pre_0, pre_1, pre_2, pre_3, factor_ref, act_ref):
    for r, pre_ref in enumerate((pre_0, pre_1, pre_2, pre_3)):
        for s in range(CAP):
            span = slice(s * N_EXP, (s + 1) * N_EXP)
            gate_pre = pre_ref[span, :HID].astype(F32)
            up_pre = pre_ref[span, HID:].astype(F32)
            sig = jax.nn.sigmoid(gate_pre)
            lift = gate_pre * sig
            factor_ref[r, span, :HID] = (up_pre * sig * (1.0 + gate_pre * (1.0 - sig))).astype(BF)
            factor_ref[r, span, HID:] = lift.astype(BF)
            act_ref[r, span, :] = (lift * up_pre).astype(BF)


def hidden_kernel(at_ref, recv_ref, down_ref, sent_ref, part_ref):
    split = split_halves()
    for r in range(GX):
        g = lax.rem(at_ref[0] + (GX - r), GX)
        for s in range(CAP):
            rows = from_pairs(recv_ref[pl.ds(g * N_EXP, N_EXP), :, s * HALF : (s + 1) * HALF])
            halves = nn(split, rows).astype(BF)
            span = slice(s * N_EXP, (s + 1) * N_EXP)
            sent_ref[r, span, :HALF] = halves[:N_EXP]
            sent_ref[r, span, HALF:] = halves[N_EXP:]
        part_ref[g] = nn(sent_ref[r], down_ref[...]).astype(BF)


def spread_kernel(part_ref, out_ref):
    total = part_ref[0].astype(F32) + part_ref[1].astype(F32)
    total = (total + (part_ref[2].astype(F32) + part_ref[3].astype(F32))).astype(BF)
    for g in range(GX):
        out_ref[g] = total


def back_kernel(at_ref, hidden_ref, factor_ref, in_ref, msg_ref):
    grads = []
    for r in range(GX):
        hidden = hidden_ref[lax.rem(at_ref[0] + (GX - r), GX)].astype(F32)
        gate_grad = (hidden * factor_ref[r, :, :HID].astype(F32)).astype(BF)
        up_grad = (hidden * factor_ref[r, :, HID:].astype(F32)).astype(BF)
        grads.append(jnp.concatenate([gate_grad, up_grad], axis=1))
    rows = nt(jnp.concatenate(grads, axis=0), in_ref[...]).astype(BF)
    join = join_halves()
    for r in range(GX):
        g = lax.rem(at_ref[0] + (GX - r), GX)
        for s in range(CAP):
            own = rows[(r * CAP + s) * N_EXP : (r * CAP + s + 1) * N_EXP]
            both = jnp.concatenate([own[:, :HALF], own[:, HALF:]], axis=0)
            msg_ref[pl.ds(g * N_EXP, N_EXP), :, s * HALF : (s + 1) * HALF] = to_pairs(nn(join, both))


def total_kernel(part_0, part_1, part_2, part_3, out_ref):
    total = part_0[...].astype(F32) + part_1[...].astype(F32)
    out_ref[...] = (total + (part_2[...].astype(F32) + part_3[...].astype(F32))).astype(BF)


def down_kernel(at_ref, sent_ref, act_ref, after_ref, out_0, out_1, out_2, out_3, full_ref):
    sent = jnp.concatenate([sent_ref[r] for r in range(GX)], axis=0)
    act = jnp.concatenate([act_ref[r] for r in range(GX)], axis=0)
    full_ref[...] = tn(sent, act).astype(BF)
    for r, out_ref in enumerate((out_0, out_1, out_2, out_3)):
        q = lax.rem(at_ref[1] + r, GY)
        out_ref[...] = full_ref[pl.ds(pl.multiple_of(q * PART, 64), PART), :]


def gather_kernel(ret_ref, ids_ref, slots_ref, out_ref):
    pick, _ = select(ids_ref, slots_ref, None)
    for g in range(GX):
        rows = jnp.concatenate(
            [
                from_pairs(ret_ref[g * N_EXP : (g + 1) * N_EXP, :, s * HALF : (s + 1) * HALF])
                for s in range(CAP)
            ],
            axis=0,
        )
        halves = tn(pick, rows).astype(BF)
        out_ref[:, g * WIDE : g * WIDE + HALF] = halves[:TOK]
        out_ref[:, g * WIDE + HALF : (g + 1) * WIDE] = halves[TOK:]


def swap(value):
    return lax.all_to_all(value, ("gx", "expert"), 0, 0, tiled=True)


def swap_gx(value):
    return lax.all_to_all(value, "gx", 0, 0, tiled=True)


def step(value, axis, r):
    return lax.ppermute(value, axis, [(i, (i + r) % 4) for i in range(4)])


def steps(value, axis):
    return [step(value, axis, r) for r in range(1, 4)]


def per_device(out_grad, route_ids, route_slots, route_probs, saved_pre, w_gate, w_up, w_down):
    ids, slots, probs = route_ids.T, route_slots.T, route_probs.T
    at = jnp.stack([lax.axis_index("gx"), lax.axis_index("gy")])
    smem = pl.BlockSpec(memory_space=pltpu.SMEM)
    vmem = pl.BlockSpec(memory_space=pltpu.VMEM)
    anywhere = pl.BlockSpec(memory_space=pl.ANY)
    message = arr(GX * N_EXP, 2, CAP * HALF)

    msg, own_down, own_in = call(
        pick_kernel,
        (message, arr(PART, HID), arr(PART, 2 * HID)),
        1 << 29,
        1 << 23,
        VMEM_MOST,
        in_specs=[anywhere] * 7,
        out_specs=[anywhere] * 3,
        scratch_shapes=[
            pltpu.VMEM((GX, TOK, WIDE), BF),
            pltpu.VMEM(ids.shape, jnp.int32),
            pltpu.VMEM(ids.shape, jnp.int32),
            pltpu.VMEM(ids.shape, F32),
            pltpu.VMEM(message.shape, BF),
            pltpu.VMEM((PART, HID), BF),
            pltpu.VMEM((PART, 2 * HID), BF),
            pltpu.SemaphoreType.DMA((GX,)),
            pltpu.SemaphoreType.DMA((3,)),
            pltpu.SemaphoreType.DMA((GX,)),
            pltpu.SemaphoreType.DMA((3,)),
            pltpu.SemaphoreType.DMA((2,)),
        ],
    )(out_grad, ids, slots, probs, w_down[0].T, w_gate[0], w_up[0])
    recv = swap(msg)

    def arrange(own):
        return call(
            arrange_kernel,
            arr(WIDE, own.shape[1]),
            0,
            1 << 23,
            in_specs=[smem] + [vmem] * 4,
        )(at, own, *steps(own, "gy"))

    down_w, in_w = arrange(own_down), arrange(own_in)
    pre = call(order_kernel, arr(ROWS, 2 * HID), 1 << 27, 1 << 21, in_specs=[vmem, anywhere])(
        saved_pre[0], msg
    )
    factors, act = call(
        factor_kernel, (arr(GX, ROWS, 2 * HID), arr(GX, ROWS, HID)), 1 << 25, 1 << 23
    )(pre, *steps(pre, "gx"))

    sent, part = call(
        hidden_kernel,
        (arr(GX, ROWS, WIDE), arr(GX, ROWS, HID)),
        1 << 31,
        1 << 23,
        in_specs=[smem, vmem, vmem],
    )(at, recv, down_w)
    hidden = swap_gx(call(spread_kernel, arr(GX, ROWS, HID), 0, 1 << 21)(swap_gx(part)))
    back = call(
        back_kernel, message, 1 << 32, 1 << 23, in_specs=[smem] + [vmem] * 3
    )(at, hidden, factors, in_w)
    ret = swap(back)

    downs = call(
        down_kernel,
        (arr(PART, HID),) * GY,
        1 << 31,
        1 << 22,
        in_specs=[smem] + [vmem] * 2 + [anywhere],
        scratch_shapes=[pltpu.VMEM((WIDE, HID), BF)],
    )(at, sent, act, back)
    grad_down = call(total_kernel, arr(PART, HID), 0, 1 << 21)(
        downs[0], *[step(downs[r], "gy", r) for r in range(1, GY)]
    )
    input_grad = call(gather_kernel, arr(TOK, GX * WIDE), 1 << 30, 1 << 22)(ret, ids, slots)
    return (input_grad, grad_down.T[None])


def solution(mesh):
    devices = mesh.devices
    grid = Mesh(devices.reshape((GX, GY) + devices.shape[1:]), ("gx", "gy", "expert"))
    rows = P(("gx", "gy", "expert"), None)
    return jax.shard_map(
        per_device,
        mesh=grid,
        in_specs=(
            rows,
            rows,
            rows,
            rows,
            P("expert", ("gx", "gy"), None),
            P("expert", ("gx", "gy"), None),
            P("expert", ("gx", "gy"), None),
            P("expert", None, ("gx", "gy")),
        ),
        out_specs=(rows, P("expert", None, ("gx", "gy"))),
        check_vma=False,
    )
```

```python
import jax
import jax.numpy as jnp
from jax import lax
from jax.experimental import pallas as pl
from jax.experimental.pallas import tpu as pltpu
from jax.sharding import Mesh, PartitionSpec as P

BF = jnp.bfloat16
F32 = jnp.float32

N_EXP = 32
CAP = 5
TOK = 128
GX = 4
GY = 4
WIDE = 1280
HALF = 640
HID = 768
ROWS = N_EXP * CAP
PAIRS = 2 * N_EXP
PART = 320
VMEM_LIMIT = 16 * 1024 * 1024
VMEM_MOST = 60 * 1024 * 1024


def iota(shape, dim):
    return lax.broadcasted_iota(jnp.int32, shape, dim)


def nn(left, right):
    return lax.dot_general(left, right, (((1,), (0,)), ((), ())), preferred_element_type=F32)


def nt(left, right):
    return lax.dot_general(left, right, (((1,), (1,)), ((), ())), preferred_element_type=F32)


def tn(left, right):
    return lax.dot_general(left, right, (((0,), (0,)), ((), ())), preferred_element_type=F32)


def one_hot(mask):
    return jnp.where(mask, 1.0, 0.0).astype(BF)


def call(body, out_shape, flops=0, moved=0, limit=VMEM_LIMIT, **kwargs):
    return pl.pallas_call(
        body,
        out_shape=out_shape,
        compiler_params=pltpu.CompilerParams(vmem_limit_bytes=limit),
        cost_estimate=pl.CostEstimate(flops=flops, bytes_accessed=moved, transcendentals=0),
        **kwargs,
    )


def arr(*dims, dtype=BF):
    return jax.ShapeDtypeStruct(dims, dtype)


def select(ids_ref, slots_ref, probs):
    code = ids_ref[...] * CAP + slots_ref[...]
    shape = (CAP * PAIRS, TOK)
    row = iota(shape, 0)
    row_code = ((row % PAIRS) // 2) * CAP + row // PAIRS
    hits = jnp.zeros(shape, F32)
    weight = jnp.zeros(shape, F32)
    for k in range(code.shape[0]):
        same = row_code == code[k : k + 1, :]
        hits = hits + jnp.where(same, 1.0, 0.0)
        if probs is not None:
            weight = weight + jnp.where(same, probs[k : k + 1, :], 0.0)
    lower = row % 2 == 0
    pick = jnp.concatenate([jnp.where(lower, hits, 0.0), jnp.where(lower, 0.0, hits)], axis=1)
    return pick.astype(BF), jnp.sum(weight, axis=1, keepdims=True)


def split_halves():
    row = iota((PAIRS, PAIRS), 0)
    col = iota((PAIRS, PAIRS), 1)
    return one_hot(col == (row % N_EXP) * 2 + row // N_EXP)


def join_halves():
    row = iota((PAIRS, PAIRS), 0)
    col = iota((PAIRS, PAIRS), 1)
    return one_hot(row == (col % N_EXP) * 2 + col // N_EXP)


def to_pairs(rows):
    return rows.reshape(N_EXP, 2, HALF).astype(BF)


def from_pairs(block):
    return block.astype(F32).reshape(PAIRS, HALF).astype(BF)


def pick_kernel(
    og_any, ids_any, slots_any, probs_any, down_any, gate_any, up_any,
    msg_any, own_down_any, own_in_any,
    og_ref, ids_ref, slots_ref, probs_ref, msg_ref, down_ref, in_ref,
    og_sem, in_sem, out_sem, fetch_sem, store_sem,
):
    small = [
        pltpu.make_async_copy(src, dst, in_sem.at[i])
        for i, (src, dst) in enumerate(((ids_any, ids_ref), (slots_any, slots_ref), (probs_any, probs_ref)))
    ]
    wide = [
        pltpu.make_async_copy(og_any.at[:, pl.ds(g * WIDE, WIDE)], og_ref.at[g], og_sem.at[g])
        for g in range(GX)
    ]
    fetches = [
        pltpu.make_async_copy(down_any, down_ref, fetch_sem.at[0]),
        pltpu.make_async_copy(gate_any, in_ref.at[:, pl.ds(0, HID)], fetch_sem.at[1]),
        pltpu.make_async_copy(up_any, in_ref.at[:, pl.ds(HID, HID)], fetch_sem.at[2]),
    ]
    stores = [
        pltpu.make_async_copy(down_ref, own_down_any, store_sem.at[0]),
        pltpu.make_async_copy(in_ref, own_in_any, store_sem.at[1]),
    ]
    for copy in small + wide + fetches:
        copy.start()
    for copy in small:
        copy.wait()
    pick, weight = select(ids_ref, slots_ref, probs_ref[...])
    sends = []
    for g in range(GX):
        wide[g].wait()
        both = jnp.concatenate([og_ref[g, :, :HALF], og_ref[g, :, HALF:]], axis=0)
        rows = nn(pick, both) * weight
        for s in range(CAP):
            msg_ref[g * N_EXP : (g + 1) * N_EXP, :, s * HALF : (s + 1) * HALF] = to_pairs(
                rows[s * PAIRS : (s + 1) * PAIRS]
            )
        span = pl.ds(g * N_EXP, N_EXP)
        sends.append(pltpu.make_async_copy(msg_ref.at[span], msg_any.at[span], out_sem.at[g]))
        sends[-1].start()
        if g == 1:
            for copy in fetches:
                copy.wait()
            for copy in stores:
                copy.start()
    for copy in sends + stores:
        copy.wait()


def arrange_kernel(at_ref, own_ref, piece_1, piece_2, piece_3, *refs):
    out_ref, token_ref = refs[-2:]
    for r, ref in enumerate((own_ref, piece_1, piece_2, piece_3)):
        q = lax.rem(at_ref[1] + (GY - r), GY)
        out_ref[pl.ds(pl.multiple_of(q * PART, 64), PART), :] = ref[...]
    token_ref[...] = jnp.zeros(token_ref.shape, F32)


def order_kernel(pre_ref, after_ref, out_ref):
    row = iota((ROWS, ROWS), 0)
    col = iota((ROWS, ROWS), 1)
    swap_rows = one_hot(col == (row % N_EXP) * CAP + row // N_EXP)
    out_ref[...] = nn(swap_rows, pre_ref[...]).astype(BF)


def factor_kernel(pre_0, pre_1, pre_2, pre_3, factor_ref, act_ref, token_ref):
    for r, pre_ref in enumerate((pre_0, pre_1, pre_2, pre_3)):
        for s in range(CAP):
            span = slice(s * N_EXP, (s + 1) * N_EXP)
            gate_pre = pre_ref[span, :HID].astype(F32)
            up_pre = pre_ref[span, HID:].astype(F32)
            sig = jax.nn.sigmoid(gate_pre)
            lift = gate_pre * sig
            factor_ref[r, span, :HID] = (up_pre * sig * (1.0 + gate_pre * (1.0 - sig))).astype(BF)
            factor_ref[r, span, HID:] = lift.astype(BF)
            act_ref[r, span, :] = (lift * up_pre).astype(BF)
    token_ref[...] = jnp.zeros(token_ref.shape, F32)


def hidden_kernel(
    at_ref, recv_any, down_any, sent_any, part_any,
    recv_ref, down_ref, sent_ref, part_ref, in_sems, down_sem, out_sems,
):
    fetches = []
    for r in range(GX):
        g = lax.rem(at_ref[0] + (GX - r), GX)
        span = pl.ds(g * N_EXP, N_EXP)
        fetches.append(pltpu.make_async_copy(recv_any.at[span], recv_ref.at[r], in_sems.at[r]))
    fetches.insert(1, pltpu.make_async_copy(down_any, down_ref, down_sem))
    for copy in fetches:
        copy.start()
    split = split_halves()
    copies = []
    for r in range(GX):
        fetches[r + (r > 0)].wait()
        for s in range(CAP):
            rows = from_pairs(recv_ref[r, :, :, s * HALF : (s + 1) * HALF])
            halves = nn(split, rows).astype(BF)
            span = slice(s * N_EXP, (s + 1) * N_EXP)
            sent_ref[r, span, :HALF] = halves[:N_EXP]
            sent_ref[r, span, HALF:] = halves[N_EXP:]
        if r == 0:
            fetches[1].wait()
        part_ref[r] = nn(sent_ref[r], down_ref[...]).astype(BF)
        g = lax.rem(at_ref[0] + (GX - r), GX)
        copies.append(pltpu.make_async_copy(part_ref.at[r], part_any.at[g], out_sems.at[0, r]))
        copies.append(pltpu.make_async_copy(sent_ref.at[r], sent_any.at[r], out_sems.at[1, r]))
        for copy in copies[-2:]:
            copy.start()
    for copy in copies:
        copy.wait()


def spread_kernel(part_ref, out_ref):
    total = part_ref[0].astype(F32) + part_ref[1].astype(F32)
    total = (total + (part_ref[2].astype(F32) + part_ref[3].astype(F32))).astype(BF)
    for g in range(GX):
        out_ref[g] = total


def back_kernel(at_ref, hidden_ref, factor_ref, in_ref, msg_any, msg_ref, sems):
    grads = []
    for r in range(GX):
        hidden = hidden_ref[lax.rem(at_ref[0] + (GX - r), GX)].astype(F32)
        gate_grad = (hidden * factor_ref[r, :, :HID].astype(F32)).astype(BF)
        up_grad = (hidden * factor_ref[r, :, HID:].astype(F32)).astype(BF)
        grads.append(jnp.concatenate([gate_grad, up_grad], axis=1))
    rows = nt(jnp.concatenate(grads, axis=0), in_ref[...]).astype(BF)
    join = join_halves()
    copies = []
    for r in range(GX):
        g = lax.rem(at_ref[0] + (GX - r), GX)
        for s in range(CAP):
            own = rows[(r * CAP + s) * N_EXP : (r * CAP + s + 1) * N_EXP]
            both = jnp.concatenate([own[:, :HALF], own[:, HALF:]], axis=0)
            msg_ref[r, :, :, s * HALF : (s + 1) * HALF] = to_pairs(nn(join, both))
        span = pl.ds(g * N_EXP, N_EXP)
        copies.append(pltpu.make_async_copy(msg_ref.at[r], msg_any.at[span], sems.at[r]))
        copies[-1].start()
    for copy in copies:
        copy.wait()


def total_kernel(part_0, part_1, part_2, part_3, out_ref):
    total = part_0[...].astype(F32) + part_1[...].astype(F32)
    out_ref[...] = (total + (part_2[...].astype(F32) + part_3[...].astype(F32))).astype(BF)


def down_kernel(at_ref, sent_ref, act_ref, after_ref, out_0, out_1, out_2, out_3, full_ref):
    sent = jnp.concatenate([sent_ref[r] for r in range(GX)], axis=0)
    act = jnp.concatenate([act_ref[r] for r in range(GX)], axis=0)
    full_ref[...] = tn(sent, act).astype(BF)
    for r, out_ref in enumerate((out_0, out_1, out_2, out_3)):
        q = lax.rem(at_ref[1] + r, GY)
        out_ref[...] = full_ref[pl.ds(pl.multiple_of(q * PART, 64), PART), :]


def gather_kernel(ret_ref, ids_ref, slots_ref, out_ref):
    pick, _ = select(ids_ref, slots_ref, None)
    for g in range(GX):
        rows = jnp.concatenate(
            [
                from_pairs(ret_ref[g * N_EXP : (g + 1) * N_EXP, :, s * HALF : (s + 1) * HALF])
                for s in range(CAP)
            ],
            axis=0,
        )
        halves = tn(pick, rows).astype(BF)
        out_ref[:, g * WIDE : g * WIDE + HALF] = halves[:TOK]
        out_ref[:, g * WIDE + HALF : (g + 1) * WIDE] = halves[TOK:]


def swap(value):
    return lax.all_to_all(value, ("gx", "expert"), 0, 0, tiled=True)


def swap_gx(value):
    return lax.all_to_all(value, "gx", 0, 0, tiled=True)


def step(value, axis, r):
    return lax.ppermute(value, axis, [(i, (i + r) % 4) for i in range(4)])


def steps(value, axis):
    return [step(value, axis, r) for r in range(1, 4)]


def per_device(out_grad, route_ids, route_slots, route_probs, saved_pre, w_gate, w_up, w_down):
    ids, slots, probs = route_ids.T, route_slots.T, route_probs.T
    at = jnp.stack([lax.axis_index("gx"), lax.axis_index("gy")])
    smem = pl.BlockSpec(memory_space=pltpu.SMEM)
    vmem = pl.BlockSpec(memory_space=pltpu.VMEM)
    anywhere = pl.BlockSpec(memory_space=pl.ANY)
    message = arr(GX * N_EXP, 2, CAP * HALF)

    msg, own_down, own_in = call(
        pick_kernel,
        (message, arr(PART, HID), arr(PART, 2 * HID)),
        1 << 29,
        1 << 23,
        VMEM_MOST,
        in_specs=[anywhere] * 7,
        out_specs=[anywhere] * 3,
        scratch_shapes=[
            pltpu.VMEM((GX, TOK, WIDE), BF),
            pltpu.VMEM(ids.shape, jnp.int32),
            pltpu.VMEM(ids.shape, jnp.int32),
            pltpu.VMEM(ids.shape, F32),
            pltpu.VMEM(message.shape, BF),
            pltpu.VMEM((PART, HID), BF),
            pltpu.VMEM((PART, 2 * HID), BF),
            pltpu.SemaphoreType.DMA((GX,)),
            pltpu.SemaphoreType.DMA((3,)),
            pltpu.SemaphoreType.DMA((GX,)),
            pltpu.SemaphoreType.DMA((3,)),
            pltpu.SemaphoreType.DMA((2,)),
        ],
    )(out_grad, ids, slots, probs, w_down[0].T, w_gate[0], w_up[0])
    recv = swap(msg)

    pre = call(order_kernel, arr(ROWS, 2 * HID), 1 << 27, 1 << 21, in_specs=[vmem, anywhere])(
        saved_pre[0], msg
    )
    token = arr(8, 128, dtype=F32)
    factors, act, factors_done = call(
        factor_kernel, (arr(GX, ROWS, 2 * HID), arr(GX, ROWS, HID), token), 1 << 25, 1 << 23, VMEM_MOST
    )(pre, *steps(pre, "gx"))

    def arrange(own, *after):
        return call(
            arrange_kernel,
            (arr(WIDE, own.shape[1]), token),
            0,
            1 << 23,
            VMEM_MOST,
            in_specs=[smem] + [vmem] * 4 + [anywhere] * len(after),
        )(at, own, *steps(own, "gy"), *after)

    in_w, in_done = arrange(own_in)
    down_w, _ = arrange(own_down, factors_done, in_done)

    sent, part = call(
        hidden_kernel,
        (arr(GX, ROWS, WIDE), arr(GX, ROWS, HID)),
        1 << 31,
        1 << 23,
        VMEM_MOST,
        in_specs=[smem, anywhere, anywhere],
        out_specs=[anywhere] * 2,
        scratch_shapes=[
            pltpu.VMEM((GX, N_EXP, 2, CAP * HALF), BF),
            pltpu.VMEM((WIDE, HID), BF),
            pltpu.VMEM((GX, ROWS, WIDE), BF),
            pltpu.VMEM((GX, ROWS, HID), BF),
            pltpu.SemaphoreType.DMA((GX,)),
            pltpu.SemaphoreType.DMA,
            pltpu.SemaphoreType.DMA((2, GX)),
        ],
    )(at, recv, down_w)
    hidden = swap_gx(call(spread_kernel, arr(GX, ROWS, HID), 0, 1 << 21)(swap_gx(part)))
    back = call(
        back_kernel,
        message,
        1 << 32,
        1 << 23,
        in_specs=[smem] + [vmem] * 3,
        out_specs=anywhere,
        scratch_shapes=[
            pltpu.VMEM((GX, N_EXP, 2, CAP * HALF), BF),
            pltpu.SemaphoreType.DMA((GX,)),
        ],
    )(at, hidden, factors, in_w)
    ret = swap(back)

    downs = call(
        down_kernel,
        (arr(PART, HID),) * GY,
        1 << 31,
        1 << 22,
        in_specs=[smem] + [vmem] * 2 + [anywhere],
        scratch_shapes=[pltpu.VMEM((WIDE, HID), BF)],
    )(at, sent, act, back)
    grad_down = call(total_kernel, arr(PART, HID), 0, 1 << 21)(
        downs[0], *[step(downs[r], "gy", r) for r in range(1, GY)]
    )
    input_grad = call(gather_kernel, arr(TOK, GX * WIDE), 1 << 30, 1 << 22)(ret, ids, slots)
    return (input_grad, grad_down.T[None])


def solution(mesh):
    devices = mesh.devices
    grid = Mesh(devices.reshape((GX, GY) + devices.shape[1:]), ("gx", "gy", "expert"))
    rows = P(("gx", "gy", "expert"), None)
    return jax.shard_map(
        per_device,
        mesh=grid,
        in_specs=(
            rows,
            rows,
            rows,
            rows,
            P("expert", ("gx", "gy"), None),
            P("expert", ("gx", "gy"), None),
            P("expert", ("gx", "gy"), None),
            P("expert", None, ("gx", "gy")),
        ),
        out_specs=(rows, P("expert", None, ("gx", "gy"))),
        check_vma=False,
    )
```

```python
import jax
import jax.numpy as jnp
from jax import lax
from jax.experimental import pallas as pl
from jax.experimental.pallas import tpu as pltpu
from jax.sharding import Mesh, PartitionSpec as P

BF = jnp.bfloat16
F32 = jnp.float32

N_EXP = 32
CAP = 5
TOK = 128
GX = 4
GY = 4
WIDE = 1280
HALF = 640
HID = 768
ROWS = N_EXP * CAP
PAIRS = 2 * N_EXP
PART = 320
VMEM_LIMIT = 16 * 1024 * 1024
VMEM_MOST = 60 * 1024 * 1024


def iota(shape, dim):
    return lax.broadcasted_iota(jnp.int32, shape, dim)


def nn(left, right):
    return lax.dot_general(left, right, (((1,), (0,)), ((), ())), preferred_element_type=F32)


def nt(left, right):
    return lax.dot_general(left, right, (((1,), (1,)), ((), ())), preferred_element_type=F32)


def tn(left, right):
    return lax.dot_general(left, right, (((0,), (0,)), ((), ())), preferred_element_type=F32)


def one_hot(mask):
    return jnp.where(mask, 1.0, 0.0).astype(BF)


def call(body, out_shape, flops=0, moved=0, limit=VMEM_LIMIT, **kwargs):
    return pl.pallas_call(
        body,
        out_shape=out_shape,
        compiler_params=pltpu.CompilerParams(vmem_limit_bytes=limit),
        cost_estimate=pl.CostEstimate(flops=flops, bytes_accessed=moved, transcendentals=0),
        **kwargs,
    )


def arr(*dims, dtype=BF):
    return jax.ShapeDtypeStruct(dims, dtype)


def select(ids_ref, slots_ref, probs):
    code = ids_ref[...] * CAP + slots_ref[...]
    shape = (CAP * PAIRS, TOK)
    row = iota(shape, 0)
    row_code = ((row % PAIRS) // 2) * CAP + row // PAIRS
    hits = jnp.zeros(shape, F32)
    weight = jnp.zeros(shape, F32)
    for k in range(code.shape[0]):
        same = row_code == code[k : k + 1, :]
        hits = hits + jnp.where(same, 1.0, 0.0)
        if probs is not None:
            weight = weight + jnp.where(same, probs[k : k + 1, :], 0.0)
    lower = row % 2 == 0
    pick = jnp.concatenate([jnp.where(lower, hits, 0.0), jnp.where(lower, 0.0, hits)], axis=1)
    return pick.astype(BF), jnp.sum(weight, axis=1, keepdims=True)


def split_halves():
    row = iota((PAIRS, PAIRS), 0)
    col = iota((PAIRS, PAIRS), 1)
    return one_hot(col == (row % N_EXP) * 2 + row // N_EXP)


def join_halves():
    row = iota((PAIRS, PAIRS), 0)
    col = iota((PAIRS, PAIRS), 1)
    return one_hot(row == (col % N_EXP) * 2 + col // N_EXP)


def to_pairs(rows):
    return rows.astype(BF).reshape(N_EXP, 2, HALF)


def from_pairs(block):
    return block.reshape(PAIRS, HALF)


def pick_kernel(
    og_any, ids_any, slots_any, probs_any, down_any, gate_any, up_any,
    msg_any, packed_any,
    og_ref, ids_ref, slots_ref, probs_ref, msg_ref, packed_ref,
    og_sem, in_sem, out_sem, fetch_sem, store_sem,
):
    small = [
        pltpu.make_async_copy(src, dst, in_sem.at[i])
        for i, (src, dst) in enumerate(((ids_any, ids_ref), (slots_any, slots_ref), (probs_any, probs_ref)))
    ]
    wide = [
        pltpu.make_async_copy(og_any.at[:, pl.ds(g * WIDE, WIDE)], og_ref.at[g], og_sem.at[g])
        for g in range(GX)
    ]
    fetches = [
        pltpu.make_async_copy(src, packed_ref.at[:, pl.ds(i * HID, HID)], fetch_sem.at[i])
        for i, src in enumerate((down_any, gate_any, up_any))
    ]
    stores = [pltpu.make_async_copy(packed_ref, packed_any, store_sem)]
    for copy in small + wide + fetches:
        copy.start()
    for copy in small:
        copy.wait()
    pick, weight = select(ids_ref, slots_ref, probs_ref[...])
    sends = []
    for g in range(GX):
        wide[g].wait()
        both = jnp.concatenate([og_ref[g, :, :HALF], og_ref[g, :, HALF:]], axis=0)
        rows = nn(pick, both) * weight
        for s in range(CAP):
            msg_ref[g * N_EXP : (g + 1) * N_EXP, :, s * HALF : (s + 1) * HALF] = to_pairs(
                rows[s * PAIRS : (s + 1) * PAIRS]
            )
        span = pl.ds(g * N_EXP, N_EXP)
        sends.append(pltpu.make_async_copy(msg_ref.at[span], msg_any.at[span], out_sem.at[g]))
        sends[-1].start()
        if g == 1:
            for copy in fetches:
                copy.wait()
            for copy in stores:
                copy.start()
    for copy in sends + stores:
        copy.wait()


def relay_kernel(less_any, more_any, after_1, after_2, after_3, low_any, high_any, low_ref, high_ref, sems):
    half = PART // 2
    copies = [
        pltpu.make_async_copy(less_any.at[pl.ds(0, half)], low_ref, sems.at[0]),
        pltpu.make_async_copy(more_any.at[pl.ds(half, half)], high_ref, sems.at[1]),
    ]
    for copy in copies:
        copy.start()
    for copy in copies:
        copy.wait()
    copies = [
        pltpu.make_async_copy(low_ref, low_any, sems.at[0]),
        pltpu.make_async_copy(high_ref, high_any, sems.at[1]),
    ]
    for copy in copies:
        copy.start()
    for copy in copies:
        copy.wait()


def arrange_kernel(at_ref, own_ref, less_ref, more_ref, far_low_ref, far_high_ref, after_ref, down_ref, in_ref):
    def put(ref, away, start):
        rows = ref.shape[0]
        q = lax.rem(at_ref[1] + away, GY)
        to = pl.ds(pl.multiple_of(q * PART + start, 32), rows)
        down_ref[to, :] = ref[:, :HID]
        in_ref[to, :] = ref[:, HID:]

    put(own_ref, 0, 0)
    put(less_ref, GY - 1, 0)
    put(more_ref, 1, 0)
    put(far_low_ref, 2, 0)
    put(far_high_ref, 2, PART // 2)


def order_kernel(pre_ref, after_ref, out_ref):
    row = iota((ROWS, ROWS), 0)
    col = iota((ROWS, ROWS), 1)
    swap_rows = one_hot(col == (row % N_EXP) * CAP + row // N_EXP)
    out_ref[...] = nn(swap_rows, pre_ref[...]).astype(BF)


def factor_kernel(pre_0, pre_1, pre_2, pre_3, factor_ref, act_ref, token_ref):
    for r, pre_ref in enumerate((pre_0, pre_1, pre_2, pre_3)):
        for s in range(CAP):
            span = slice(s * N_EXP, (s + 1) * N_EXP)
            gate_pre = pre_ref[span, :HID].astype(F32)
            up_pre = pre_ref[span, HID:].astype(F32)
            sig = jax.nn.sigmoid(gate_pre)
            lift = gate_pre * sig
            factor_ref[r, span, :HID] = (up_pre * sig * (1.0 + gate_pre * (1.0 - sig))).astype(BF)
            factor_ref[r, span, HID:] = lift.astype(BF)
            act_ref[r, span, :] = (lift * up_pre).astype(BF)
    token_ref[...] = jnp.zeros(token_ref.shape, F32)


def put_rows(split, block_of, sent_ref, r):
    for s in range(CAP):
        rows = from_pairs(block_of(slice(s * HALF, (s + 1) * HALF)))
        halves = nn(split, rows).astype(BF)
        span = slice(s * N_EXP, (s + 1) * N_EXP)
        sent_ref[r, span, :HALF] = halves[:N_EXP]
        sent_ref[r, span, HALF:] = halves[N_EXP:]


def hidden_kernel(
    at_ref, recv_any, down_any, part_any,
    recv_ref, down_ref, sent_ref, part_ref, in_sems, down_sem, out_sems,
):
    fetches = []
    for r in range(GX):
        g = lax.rem(at_ref[0] + (GX - r), GX)
        span = pl.ds(g * N_EXP, N_EXP)
        fetches.append(pltpu.make_async_copy(recv_any.at[span], recv_ref.at[r], in_sems.at[r]))
    fetches.insert(1, pltpu.make_async_copy(down_any, down_ref, down_sem))
    for copy in fetches:
        copy.start()
    split = split_halves()
    copies = []
    for r in range(GX):
        fetches[r + (r > 0)].wait()
        put_rows(split, lambda cols: recv_ref[r, :, :, cols], sent_ref, r)
        if r == 0:
            fetches[1].wait()
        part_ref[r] = nn(sent_ref[r], down_ref[...]).astype(BF)
        g = lax.rem(at_ref[0] + (GX - r), GX)
        copies.append(pltpu.make_async_copy(part_ref.at[r], part_any.at[g], out_sems.at[r]))
        copies[-1].start()
    for copy in copies:
        copy.wait()


def spread_kernel(part_ref, out_ref):
    total = part_ref[0].astype(F32) + part_ref[1].astype(F32)
    total = (total + (part_ref[2].astype(F32) + part_ref[3].astype(F32))).astype(BF)
    for g in range(GX):
        out_ref[g] = total


def back_kernel(at_ref, hidden_ref, factor_ref, in_ref, msg_any, msg_ref, sems):
    grads = []
    for r in range(GX):
        hidden = hidden_ref[lax.rem(at_ref[0] + (GX - r), GX)].astype(F32)
        gate_grad = (hidden * factor_ref[r, :, :HID].astype(F32)).astype(BF)
        up_grad = (hidden * factor_ref[r, :, HID:].astype(F32)).astype(BF)
        grads.append(jnp.concatenate([gate_grad, up_grad], axis=1))
    rows = nt(jnp.concatenate(grads, axis=0), in_ref[...]).astype(BF)
    join = join_halves()
    copies = []
    for r in range(GX):
        g = lax.rem(at_ref[0] + (GX - r), GX)
        for s in range(CAP):
            own = rows[(r * CAP + s) * N_EXP : (r * CAP + s + 1) * N_EXP]
            both = jnp.concatenate([own[:, :HALF], own[:, HALF:]], axis=0)
            msg_ref[r, :, :, s * HALF : (s + 1) * HALF] = to_pairs(nn(join, both))
        span = pl.ds(g * N_EXP, N_EXP)
        copies.append(pltpu.make_async_copy(msg_ref.at[r], msg_any.at[span], sems.at[r]))
        copies[-1].start()
    for copy in copies:
        copy.wait()


def total_kernel(part_0, part_1, part_2, part_3, out_ref):
    total = part_0[...].astype(F32) + part_1[...].astype(F32)
    out_ref[...] = (total + (part_2[...].astype(F32) + part_3[...].astype(F32))).astype(BF)


def down_kernel(at_ref, recv_ref, act_ref, after_ref, out_0, out_1, out_2, out_3, sent_ref, full_ref):
    split = split_halves()
    for r in range(GX):
        span = pl.ds(lax.rem(at_ref[0] + (GX - r), GX) * N_EXP, N_EXP)
        put_rows(split, lambda cols: recv_ref[span, :, cols], sent_ref, r)
    sent = jnp.concatenate([sent_ref[r] for r in range(GX)], axis=0)
    act = jnp.concatenate([act_ref[r] for r in range(GX)], axis=0)
    full_ref[...] = tn(sent, act).astype(BF)
    for r, out_ref in enumerate((out_0, out_1, out_2, out_3)):
        q = lax.rem(at_ref[1] + r, GY)
        out_ref[...] = full_ref[pl.ds(pl.multiple_of(q * PART, 64), PART), :]


def gather_kernel(ret_ref, ids_ref, slots_ref, out_ref):
    pick, _ = select(ids_ref, slots_ref, None)
    for g in range(GX):
        rows = jnp.concatenate(
            [
                from_pairs(ret_ref[g * N_EXP : (g + 1) * N_EXP, :, s * HALF : (s + 1) * HALF])
                for s in range(CAP)
            ],
            axis=0,
        )
        halves = tn(pick, rows).astype(BF)
        out_ref[:, g * WIDE : g * WIDE + HALF] = halves[:TOK]
        out_ref[:, g * WIDE + HALF : (g + 1) * WIDE] = halves[TOK:]


def swap(value):
    return lax.all_to_all(value, ("gx", "expert"), 0, 0, tiled=True)


def swap_gx(value):
    return lax.all_to_all(value, "gx", 0, 0, tiled=True)


def step(value, axis, r):
    return lax.ppermute(value, axis, [(i, (i + r) % 4) for i in range(4)])


def steps(value, axis):
    return [step(value, axis, r) for r in range(1, 4)]


def per_device(out_grad, route_ids, route_slots, route_probs, saved_pre, w_gate, w_up, w_down):
    ids, slots, probs = route_ids.T, route_slots.T, route_probs.T
    at = jnp.stack([lax.axis_index("gx"), lax.axis_index("gy")])
    smem = pl.BlockSpec(memory_space=pltpu.SMEM)
    vmem = pl.BlockSpec(memory_space=pltpu.VMEM)
    anywhere = pl.BlockSpec(memory_space=pl.ANY)
    message = arr(GX * N_EXP, 2, CAP * HALF)

    msg, packed = call(
        pick_kernel,
        (message, arr(PART, 3 * HID)),
        1 << 29,
        1 << 23,
        VMEM_MOST,
        in_specs=[anywhere] * 7,
        out_specs=[anywhere] * 2,
        scratch_shapes=[
            pltpu.VMEM((GX, TOK, WIDE), BF),
            pltpu.VMEM(ids.shape, jnp.int32),
            pltpu.VMEM(ids.shape, jnp.int32),
            pltpu.VMEM(ids.shape, F32),
            pltpu.VMEM(message.shape, BF),
            pltpu.VMEM((PART, 3 * HID), BF),
            pltpu.SemaphoreType.DMA((GX,)),
            pltpu.SemaphoreType.DMA((3,)),
            pltpu.SemaphoreType.DMA((GX,)),
            pltpu.SemaphoreType.DMA((3,)),
            pltpu.SemaphoreType.DMA,
        ],
    )(out_grad, ids, slots, probs, w_down[0].T, w_gate[0], w_up[0])
    recv = swap(msg)

    pre = call(order_kernel, arr(ROWS, 2 * HID), 1 << 27, 1 << 21, in_specs=[vmem, anywhere])(
        saved_pre[0], msg
    )
    pres = steps(pre, "gx")
    less, more = step(packed, "gy", 1), step(packed, "gy", 3)
    half = arr(PART // 2, 3 * HID)
    low, high = call(
        relay_kernel,
        (half, half),
        0,
        1 << 22,
        in_specs=[anywhere] * 5,
        out_specs=[anywhere] * 2,
        scratch_shapes=[
            pltpu.VMEM(half.shape, BF),
            pltpu.VMEM(half.shape, BF),
            pltpu.SemaphoreType.DMA((2,)),
        ],
    )(less, more, *pres)
    factors, act, factors_done = call(
        factor_kernel,
        (arr(GX, ROWS, 2 * HID), arr(GX, ROWS, HID), arr(8, 128, dtype=F32)),
        1 << 25,
        1 << 23,
        VMEM_MOST,
    )(pre, *pres)
    down_w, in_w = call(
        arrange_kernel,
        (arr(WIDE, HID), arr(WIDE, 2 * HID)),
        0,
        1 << 24,
        VMEM_MOST,
        in_specs=[smem] + [vmem] * 5 + [anywhere],
    )(at, packed, less, more, step(low, "gy", 1), step(high, "gy", 3), factors_done)

    part = call(
        hidden_kernel,
        arr(GX, ROWS, HID),
        1 << 31,
        1 << 23,
        VMEM_MOST,
        in_specs=[smem, anywhere, anywhere],
        out_specs=anywhere,
        scratch_shapes=[
            pltpu.VMEM((GX, N_EXP, 2, CAP * HALF), BF),
            pltpu.VMEM((WIDE, HID), BF),
            pltpu.VMEM((GX, ROWS, WIDE), BF),
            pltpu.VMEM((GX, ROWS, HID), BF),
            pltpu.SemaphoreType.DMA((GX,)),
            pltpu.SemaphoreType.DMA,
            pltpu.SemaphoreType.DMA((GX,)),
        ],
    )(at, recv, down_w)
    hidden = swap_gx(call(spread_kernel, arr(GX, ROWS, HID), 0, 1 << 21)(swap_gx(part)))
    back = call(
        back_kernel,
        message,
        1 << 32,
        1 << 23,
        in_specs=[smem] + [vmem] * 3,
        out_specs=anywhere,
        scratch_shapes=[
            pltpu.VMEM((GX, N_EXP, 2, CAP * HALF), BF),
            pltpu.SemaphoreType.DMA((GX,)),
        ],
    )(at, hidden, factors, in_w)
    ret = swap(back)

    downs = call(
        down_kernel,
        (arr(PART, HID),) * GY,
        1 << 31,
        1 << 22,
        in_specs=[smem] + [vmem] * 2 + [anywhere],
        scratch_shapes=[pltpu.VMEM((GX, ROWS, WIDE), BF), pltpu.VMEM((WIDE, HID), BF)],
    )(at, recv, act, back)
    grad_down = call(total_kernel, arr(PART, HID), 0, 1 << 21)(
        downs[0], *[step(downs[r], "gy", r) for r in range(1, GY)]
    )
    input_grad = call(gather_kernel, arr(TOK, GX * WIDE), 1 << 30, 1 << 22)(ret, ids, slots)
    return (input_grad, grad_down.T[None])


def solution(mesh):
    devices = mesh.devices
    grid = Mesh(devices.reshape((GX, GY) + devices.shape[1:]), ("gx", "gy", "expert"))
    rows = P(("gx", "gy", "expert"), None)
    return jax.shard_map(
        per_device,
        mesh=grid,
        in_specs=(
            rows,
            rows,
            rows,
            rows,
            P("expert", ("gx", "gy"), None),
            P("expert", ("gx", "gy"), None),
            P("expert", ("gx", "gy"), None),
            P("expert", None, ("gx", "gy")),
        ),
        out_specs=(rows, P("expert", None, ("gx", "gy"))),
        check_vma=False,
    )
```

```python
import functools

import jax
import jax.numpy as jnp
from jax import lax
from jax.experimental import pallas as pl
from jax.experimental.pallas import tpu as pltpu
from jax.sharding import Mesh, PartitionSpec as P

BF = jnp.bfloat16
F32 = jnp.float32

N_EXP = 32
CAP = 5
TOK = 128
GX = 4
GY = 4
WIDE = 1280
HALF = 640
HID = 768
ROWS = N_EXP * CAP
PAIRS = 2 * N_EXP
PART = 320
VMEM_LIMIT = 16 * 1024 * 1024
VMEM_MOST = 60 * 1024 * 1024


def iota(shape, dim):
    return lax.broadcasted_iota(jnp.int32, shape, dim)


def nn(left, right):
    return lax.dot_general(left, right, (((1,), (0,)), ((), ())), preferred_element_type=F32)


def nt(left, right):
    return lax.dot_general(left, right, (((1,), (1,)), ((), ())), preferred_element_type=F32)


def tn(left, right):
    return lax.dot_general(left, right, (((0,), (0,)), ((), ())), preferred_element_type=F32)


def one_hot(mask):
    return jnp.where(mask, 1.0, 0.0).astype(BF)


def call(body, out_shape, flops=0, moved=0, limit=VMEM_LIMIT, **kwargs):
    return pl.pallas_call(
        body,
        out_shape=out_shape,
        compiler_params=pltpu.CompilerParams(vmem_limit_bytes=limit),
        cost_estimate=pl.CostEstimate(flops=flops, bytes_accessed=moved, transcendentals=0),
        **kwargs,
    )


def arr(*dims, dtype=BF):
    return jax.ShapeDtypeStruct(dims, dtype)


def select(ids_ref, slots_ref, probs):
    code = ids_ref[...] * CAP + slots_ref[...]
    shape = (CAP * PAIRS, TOK)
    row = iota(shape, 0)
    row_code = ((row % PAIRS) // 2) * CAP + row // PAIRS
    hits = jnp.zeros(shape, F32)
    weight = jnp.zeros(shape, F32)
    for k in range(code.shape[0]):
        same = row_code == code[k : k + 1, :]
        hits = hits + jnp.where(same, 1.0, 0.0)
        if probs is not None:
            weight = weight + jnp.where(same, probs[k : k + 1, :], 0.0)
    lower = row % 2 == 0
    pick = jnp.concatenate([jnp.where(lower, hits, 0.0), jnp.where(lower, 0.0, hits)], axis=1)
    return pick.astype(BF), jnp.sum(weight, axis=1, keepdims=True)


def split_halves():
    row = iota((PAIRS, PAIRS), 0)
    col = iota((PAIRS, PAIRS), 1)
    return one_hot(col == (row % N_EXP) * 2 + row // N_EXP)


def join_halves():
    row = iota((PAIRS, PAIRS), 0)
    col = iota((PAIRS, PAIRS), 1)
    return one_hot(row == (col % N_EXP) * 2 + col // N_EXP)


def to_pairs(rows):
    return rows.astype(BF).reshape(N_EXP, 2, HALF)


def from_pairs(block):
    return block.reshape(PAIRS, HALF)


def pick_kernel(
    og_any, ids_any, slots_any, probs_any, down_any, gate_any, up_any,
    msg_any, packed_any,
    og_ref, ids_ref, slots_ref, probs_ref, msg_ref, packed_ref,
    og_sem, in_sem, out_sem, fetch_sem, store_sem,
):
    small = [
        pltpu.make_async_copy(src, dst, in_sem.at[i])
        for i, (src, dst) in enumerate(((ids_any, ids_ref), (slots_any, slots_ref), (probs_any, probs_ref)))
    ]
    wide = [
        pltpu.make_async_copy(og_any.at[:, pl.ds(g * WIDE, WIDE)], og_ref.at[g], og_sem.at[g])
        for g in range(GX)
    ]
    fetches = [
        pltpu.make_async_copy(src, packed_ref.at[:, pl.ds(i * HID, HID)], fetch_sem.at[i])
        for i, src in enumerate((down_any, gate_any, up_any))
    ]
    stores = [pltpu.make_async_copy(packed_ref, packed_any, store_sem)]
    for copy in small + wide + fetches:
        copy.start()
    for copy in small:
        copy.wait()
    pick, weight = select(ids_ref, slots_ref, probs_ref[...])
    sends = []
    for g in range(GX):
        wide[g].wait()
        both = jnp.concatenate([og_ref[g, :, :HALF], og_ref[g, :, HALF:]], axis=0)
        rows = nn(pick, both) * weight
        for s in range(CAP):
            msg_ref[g * N_EXP : (g + 1) * N_EXP, :, s * HALF : (s + 1) * HALF] = to_pairs(
                rows[s * PAIRS : (s + 1) * PAIRS]
            )
        span = pl.ds(g * N_EXP, N_EXP)
        sends.append(pltpu.make_async_copy(msg_ref.at[span], msg_any.at[span], out_sem.at[g]))
        sends[-1].start()
        if g == 1:
            for copy in fetches:
                copy.wait()
            for copy in stores:
                copy.start()
    for copy in sends + stores:
        copy.wait()


def relay_kernel(less_any, more_any, after_1, after_2, after_3, low_any, high_any, low_ref, high_ref, sems):
    half = PART // 2
    copies = [
        pltpu.make_async_copy(less_any.at[pl.ds(0, half)], low_ref, sems.at[0]),
        pltpu.make_async_copy(more_any.at[pl.ds(half, half)], high_ref, sems.at[1]),
    ]
    for copy in copies:
        copy.start()
    for copy in copies:
        copy.wait()
    copies = [
        pltpu.make_async_copy(low_ref, low_any, sems.at[0]),
        pltpu.make_async_copy(high_ref, high_any, sems.at[1]),
    ]
    for copy in copies:
        copy.start()
    for copy in copies:
        copy.wait()


def arrange_kernel(places, at_ref, *refs):
    pieces, (down_any, in_any, sems) = refs[: len(places)], refs[-3:]
    copies = []
    for i, (ref, (away, start)) in enumerate(zip(pieces, places)):
        q = lax.rem(at_ref[1] + away, GY)
        to = pl.ds(pl.multiple_of(q * PART + start, 32), ref.shape[0])
        copies.append(pltpu.make_async_copy(ref.at[:, pl.ds(0, HID)], down_any.at[to], sems.at[0, i]))
        copies.append(pltpu.make_async_copy(ref.at[:, pl.ds(HID, 2 * HID)], in_any.at[to], sems.at[1, i]))
    for copy in copies:
        copy.start()
    for copy in copies:
        copy.wait()


def order_kernel(pre_ref, after_ref, out_ref):
    row = iota((ROWS, ROWS), 0)
    col = iota((ROWS, ROWS), 1)
    swap_rows = one_hot(col == (row % N_EXP) * CAP + row // N_EXP)
    out_ref[...] = nn(swap_rows, pre_ref[...]).astype(BF)


def factor_kernel(pre_0, pre_1, pre_2, pre_3, factor_ref, act_ref, token_ref):
    for r, pre_ref in enumerate((pre_0, pre_1, pre_2, pre_3)):
        for s in range(CAP):
            span = slice(s * N_EXP, (s + 1) * N_EXP)
            gate_pre = pre_ref[span, :HID].astype(F32)
            up_pre = pre_ref[span, HID:].astype(F32)
            sig = jax.nn.sigmoid(gate_pre)
            lift = gate_pre * sig
            factor_ref[r, span, :HID] = (up_pre * sig * (1.0 + gate_pre * (1.0 - sig))).astype(BF)
            factor_ref[r, span, HID:] = lift.astype(BF)
            act_ref[r, span, :] = (lift * up_pre).astype(BF)
    token_ref[...] = jnp.zeros(token_ref.shape, F32)


def put_rows(split, block_of, sent_ref, r):
    for s in range(CAP):
        rows = from_pairs(block_of(slice(s * HALF, (s + 1) * HALF)))
        halves = nn(split, rows).astype(BF)
        span = slice(s * N_EXP, (s + 1) * N_EXP)
        sent_ref[r, span, :HALF] = halves[:N_EXP]
        sent_ref[r, span, HALF:] = halves[N_EXP:]


def hidden_kernel(
    at_ref, recv_any, down_any, part_any,
    recv_ref, down_ref, sent_ref, part_ref, in_sems, down_sem, out_sems,
):
    fetches = []
    for r in range(GX):
        span = pl.ds(lax.rem(at_ref[0] + (GX - r), GX) * N_EXP, N_EXP)
        fetches.append(pltpu.make_async_copy(recv_any.at[span], recv_ref.at[r], in_sems.at[r]))
    fetches.append(pltpu.make_async_copy(down_any, down_ref, down_sem))
    for copy in fetches:
        copy.start()
    split = split_halves()
    for r in range(GX):
        fetches[r].wait()
        put_rows(split, lambda cols: recv_ref[r, :, :, cols], sent_ref, r)
    fetches[GX].wait()
    copies = []
    for pair in range(2):
        sent = jnp.concatenate([sent_ref[2 * pair], sent_ref[2 * pair + 1]], axis=0)
        part = nn(sent, down_ref[...]).astype(BF)
        for r in (2 * pair, 2 * pair + 1):
            part_ref[r] = part[(r % 2) * ROWS : (r % 2 + 1) * ROWS]
            g = lax.rem(at_ref[0] + (GX - r), GX)
            copies.append(pltpu.make_async_copy(part_ref.at[r], part_any.at[g], out_sems.at[r]))
            copies[-1].start()
    for copy in copies:
        copy.wait()


def spread_kernel(part_ref, out_ref):
    total = part_ref[0].astype(F32) + part_ref[1].astype(F32)
    total = (total + (part_ref[2].astype(F32) + part_ref[3].astype(F32))).astype(BF)
    for g in range(GX):
        out_ref[g] = total


def back_kernel(at_ref, hidden_ref, factor_ref, in_ref, msg_any, msg_ref, sems):
    grads = []
    for r in range(GX):
        hidden = hidden_ref[lax.rem(at_ref[0] + (GX - r), GX)].astype(F32)
        gate_grad = (hidden * factor_ref[r, :, :HID].astype(F32)).astype(BF)
        up_grad = (hidden * factor_ref[r, :, HID:].astype(F32)).astype(BF)
        grads.append(jnp.concatenate([gate_grad, up_grad], axis=1))
    rows = nt(jnp.concatenate(grads, axis=0), in_ref[...]).astype(BF)
    join = join_halves()
    copies = []
    for r in range(GX):
        g = lax.rem(at_ref[0] + (GX - r), GX)
        for s in range(CAP):
            own = rows[(r * CAP + s) * N_EXP : (r * CAP + s + 1) * N_EXP]
            both = jnp.concatenate([own[:, :HALF], own[:, HALF:]], axis=0)
            msg_ref[r, :, :, s * HALF : (s + 1) * HALF] = to_pairs(nn(join, both))
        span = pl.ds(g * N_EXP, N_EXP)
        copies.append(pltpu.make_async_copy(msg_ref.at[r], msg_any.at[span], sems.at[r]))
        copies[-1].start()
    for copy in copies:
        copy.wait()


def total_kernel(part_0, part_1, part_2, part_3, out_ref):
    total = part_0[...].astype(F32) + part_1[...].astype(F32)
    out_ref[...] = (total + (part_2[...].astype(F32) + part_3[...].astype(F32))).astype(BF)


def down_kernel(at_ref, recv_ref, act_ref, after_ref, out_0, out_1, out_2, out_3, sent_ref, full_ref):
    split = split_halves()
    for r in range(GX):
        span = pl.ds(lax.rem(at_ref[0] + (GX - r), GX) * N_EXP, N_EXP)
        put_rows(split, lambda cols: recv_ref[span, :, cols], sent_ref, r)
    sent = jnp.concatenate([sent_ref[r] for r in range(GX)], axis=0)
    act = jnp.concatenate([act_ref[r] for r in range(GX)], axis=0)
    full_ref[...] = tn(sent, act).astype(BF)
    for r, out_ref in enumerate((out_0, out_1, out_2, out_3)):
        q = lax.rem(at_ref[1] + r, GY)
        out_ref[...] = full_ref[pl.ds(pl.multiple_of(q * PART, 64), PART), :]


def gather_kernel(ret_ref, ids_ref, slots_ref, out_ref):
    pick, _ = select(ids_ref, slots_ref, None)
    for g in range(GX):
        rows = jnp.concatenate(
            [
                from_pairs(ret_ref[g * N_EXP : (g + 1) * N_EXP, :, s * HALF : (s + 1) * HALF])
                for s in range(CAP)
            ],
            axis=0,
        )
        halves = tn(pick, rows).astype(BF)
        out_ref[:, g * WIDE : g * WIDE + HALF] = halves[:TOK]
        out_ref[:, g * WIDE + HALF : (g + 1) * WIDE] = halves[TOK:]


def swap(value):
    return lax.all_to_all(value, ("gx", "expert"), 0, 0, tiled=True)


def swap_gx(value):
    return lax.all_to_all(value, "gx", 0, 0, tiled=True)


def step(value, axis, r):
    return lax.ppermute(value, axis, [(i, (i + r) % 4) for i in range(4)])


def steps(value, axis):
    return [step(value, axis, r) for r in range(1, 4)]


def per_device(out_grad, route_ids, route_slots, route_probs, saved_pre, w_gate, w_up, w_down):
    ids, slots, probs = route_ids.T, route_slots.T, route_probs.T
    at = jnp.stack([lax.axis_index("gx"), lax.axis_index("gy")])
    smem = pl.BlockSpec(memory_space=pltpu.SMEM)
    vmem = pl.BlockSpec(memory_space=pltpu.VMEM)
    anywhere = pl.BlockSpec(memory_space=pl.ANY)
    message = arr(GX * N_EXP, 2, CAP * HALF)

    msg, packed = call(
        pick_kernel,
        (message, arr(PART, 3 * HID)),
        1 << 29,
        1 << 23,
        VMEM_MOST,
        in_specs=[anywhere] * 7,
        out_specs=[anywhere] * 2,
        scratch_shapes=[
            pltpu.VMEM((GX, TOK, WIDE), BF),
            pltpu.VMEM(ids.shape, jnp.int32),
            pltpu.VMEM(ids.shape, jnp.int32),
            pltpu.VMEM(ids.shape, F32),
            pltpu.VMEM(message.shape, BF),
            pltpu.VMEM((PART, 3 * HID), BF),
            pltpu.SemaphoreType.DMA((GX,)),
            pltpu.SemaphoreType.DMA((3,)),
            pltpu.SemaphoreType.DMA((GX,)),
            pltpu.SemaphoreType.DMA((3,)),
            pltpu.SemaphoreType.DMA,
        ],
    )(out_grad, ids, slots, probs, w_down[0].T, w_gate[0], w_up[0])
    recv = swap(msg)

    pre = call(order_kernel, arr(ROWS, 2 * HID), 1 << 27, 1 << 21, in_specs=[vmem, anywhere])(
        saved_pre[0], msg
    )
    pres = steps(pre, "gx")
    less, more = step(packed, "gy", 1), step(packed, "gy", 3)
    half = arr(PART // 2, 3 * HID)
    low, high = call(
        relay_kernel,
        (half, half),
        0,
        1 << 22,
        in_specs=[anywhere] * 5,
        out_specs=[anywhere] * 2,
        scratch_shapes=[
            pltpu.VMEM(half.shape, BF),
            pltpu.VMEM(half.shape, BF),
            pltpu.SemaphoreType.DMA((2,)),
        ],
    )(less, more, *pres)
    factors, act, factors_done = call(
        factor_kernel,
        (arr(GX, ROWS, 2 * HID), arr(GX, ROWS, HID), arr(8, 128, dtype=F32)),
        1 << 25,
        1 << 23,
        VMEM_MOST,
    )(pre, *pres)
    def arrange(places, pieces, others, aliases):
        return call(
            functools.partial(arrange_kernel, places),
            (arr(WIDE, HID), arr(WIDE, 2 * HID)),
            0,
            1 << 24,
            VMEM_MOST,
            in_specs=[smem] + [vmem] * len(pieces) + [anywhere] * len(others),
            out_specs=[anywhere] * 2,
            scratch_shapes=[pltpu.SemaphoreType.DMA((2, len(places)))],
            input_output_aliases=aliases,
        )(at, *pieces, *others)

    near = arrange(((0, 0), (GY - 1, 0), (1, 0)), (packed, less, more), (), {})
    down_w, in_w = arrange(
        ((2, 0), (2, PART // 2)),
        (step(low, "gy", 1), step(high, "gy", 3)),
        (*near, factors_done),
        {3: 0, 4: 1},
    )

    part = call(
        hidden_kernel,
        arr(GX, ROWS, HID),
        1 << 31,
        1 << 23,
        VMEM_MOST,
        in_specs=[smem, anywhere, anywhere],
        out_specs=anywhere,
        scratch_shapes=[
            pltpu.VMEM((GX, N_EXP, 2, CAP * HALF), BF),
            pltpu.VMEM((WIDE, HID), BF),
            pltpu.VMEM((GX, ROWS, WIDE), BF),
            pltpu.VMEM((GX, ROWS, HID), BF),
            pltpu.SemaphoreType.DMA((GX,)),
            pltpu.SemaphoreType.DMA,
            pltpu.SemaphoreType.DMA((GX,)),
        ],
    )(at, recv, down_w)
    hidden = swap_gx(call(spread_kernel, arr(GX, ROWS, HID), 0, 1 << 21)(swap_gx(part)))
    back = call(
        back_kernel,
        message,
        1 << 32,
        1 << 23,
        in_specs=[smem] + [vmem] * 3,
        out_specs=anywhere,
        scratch_shapes=[
            pltpu.VMEM((GX, N_EXP, 2, CAP * HALF), BF),
            pltpu.SemaphoreType.DMA((GX,)),
        ],
    )(at, hidden, factors, in_w)
    ret = swap(back)

    downs = call(
        down_kernel,
        (arr(PART, HID),) * GY,
        1 << 31,
        1 << 22,
        in_specs=[smem] + [vmem] * 2 + [anywhere],
        scratch_shapes=[pltpu.VMEM((GX, ROWS, WIDE), BF), pltpu.VMEM((WIDE, HID), BF)],
    )(at, recv, act, back)
    grad_down = call(total_kernel, arr(PART, HID), 0, 1 << 21)(
        downs[0], *[step(downs[r], "gy", r) for r in range(1, GY)]
    )
    input_grad = call(gather_kernel, arr(TOK, GX * WIDE), 1 << 30, 1 << 22)(ret, ids, slots)
    return (input_grad, grad_down.T[None])


def solution(mesh):
    devices = mesh.devices
    grid = Mesh(devices.reshape((GX, GY) + devices.shape[1:]), ("gx", "gy", "expert"))
    rows = P(("gx", "gy", "expert"), None)
    return jax.shard_map(
        per_device,
        mesh=grid,
        in_specs=(
            rows,
            rows,
            rows,
            rows,
            P("expert", ("gx", "gy"), None),
            P("expert", ("gx", "gy"), None),
            P("expert", ("gx", "gy"), None),
            P("expert", None, ("gx", "gy")),
        ),
        out_specs=(rows, P("expert", None, ("gx", "gy"))),
        check_vma=False,
    )
```

```python
import functools

import jax
import jax.numpy as jnp
from jax import lax
from jax.experimental import pallas as pl
from jax.experimental.pallas import tpu as pltpu
from jax.sharding import Mesh, PartitionSpec as P

BF = jnp.bfloat16
F32 = jnp.float32

N_EXP = 32
CAP = 5
TOK = 128
GX = 4
GY = 4
WIDE = 1280
HALF = 640
HID = 768
ROWS = N_EXP * CAP
PAIRS = 2 * N_EXP
PART = 320
VMEM_LIMIT = 16 * 1024 * 1024
VMEM_MOST = 60 * 1024 * 1024


def iota(shape, dim):
    return lax.broadcasted_iota(jnp.int32, shape, dim)


def nn(left, right):
    return lax.dot_general(left, right, (((1,), (0,)), ((), ())), preferred_element_type=F32)


def nt(left, right):
    return lax.dot_general(left, right, (((1,), (1,)), ((), ())), preferred_element_type=F32)


def tn(left, right):
    return lax.dot_general(left, right, (((0,), (0,)), ((), ())), preferred_element_type=F32)


def one_hot(mask):
    return jnp.where(mask, 1.0, 0.0).astype(BF)


def call(body, out_shape, flops=0, moved=0, limit=VMEM_LIMIT, **kwargs):
    return pl.pallas_call(
        body,
        out_shape=out_shape,
        compiler_params=pltpu.CompilerParams(vmem_limit_bytes=limit),
        cost_estimate=pl.CostEstimate(flops=flops, bytes_accessed=moved, transcendentals=0),
        **kwargs,
    )


def arr(*dims, dtype=BF):
    return jax.ShapeDtypeStruct(dims, dtype)


def select(ids_ref, slots_ref, probs):
    code = ids_ref[...] * CAP + slots_ref[...]
    shape = (CAP * PAIRS, TOK)
    row = iota(shape, 0)
    row_code = ((row % PAIRS) // 2) * CAP + row // PAIRS
    hits = jnp.zeros(shape, F32)
    weight = jnp.zeros(shape, F32)
    for k in range(code.shape[0]):
        same = row_code == code[k : k + 1, :]
        hits = hits + jnp.where(same, 1.0, 0.0)
        if probs is not None:
            weight = weight + jnp.where(same, probs[k : k + 1, :], 0.0)
    lower = row % 2 == 0
    pick = jnp.concatenate([jnp.where(lower, hits, 0.0), jnp.where(lower, 0.0, hits)], axis=1)
    return pick.astype(BF), jnp.sum(weight, axis=1, keepdims=True)


def split_halves():
    row = iota((PAIRS, PAIRS), 0)
    col = iota((PAIRS, PAIRS), 1)
    return one_hot(col == (row % N_EXP) * 2 + row // N_EXP)


def join_halves():
    row = iota((PAIRS, PAIRS), 0)
    col = iota((PAIRS, PAIRS), 1)
    return one_hot(row == (col % N_EXP) * 2 + col // N_EXP)


def to_pairs(rows):
    return rows.astype(BF).reshape(N_EXP, 2, HALF)


def from_pairs(block):
    return block.reshape(PAIRS, HALF)


def pick_kernel(
    og_any, ids_any, slots_any, probs_any, down_any, gate_any, up_any,
    msg_any, packed_any,
    og_ref, ids_ref, slots_ref, probs_ref, msg_ref, packed_ref,
    og_sem, in_sem, out_sem, fetch_sem, store_sem,
):
    small = [
        pltpu.make_async_copy(src, dst, in_sem.at[i])
        for i, (src, dst) in enumerate(((ids_any, ids_ref), (slots_any, slots_ref), (probs_any, probs_ref)))
    ]
    wide = [
        pltpu.make_async_copy(og_any.at[:, pl.ds(g * WIDE, WIDE)], og_ref.at[g], og_sem.at[g])
        for g in range(GX)
    ]
    fetches = [
        pltpu.make_async_copy(src, packed_ref.at[:, pl.ds(i * HID, HID)], fetch_sem.at[i])
        for i, src in enumerate((down_any, gate_any, up_any))
    ]
    stores = [pltpu.make_async_copy(packed_ref, packed_any, store_sem)]
    for copy in small + wide + fetches:
        copy.start()
    for copy in small:
        copy.wait()
    pick, weight = select(ids_ref, slots_ref, probs_ref[...])
    sends = []
    for g in range(GX):
        wide[g].wait()
        both = jnp.concatenate([og_ref[g, :, :HALF], og_ref[g, :, HALF:]], axis=0)
        rows = nn(pick, both) * weight
        for s in range(CAP):
            msg_ref[g * N_EXP : (g + 1) * N_EXP, :, s * HALF : (s + 1) * HALF] = to_pairs(
                rows[s * PAIRS : (s + 1) * PAIRS]
            )
        span = pl.ds(g * N_EXP, N_EXP)
        sends.append(pltpu.make_async_copy(msg_ref.at[span], msg_any.at[span], out_sem.at[g]))
        sends[-1].start()
        if g == 1:
            for copy in fetches:
                copy.wait()
            for copy in stores:
                copy.start()
    for copy in sends + stores:
        copy.wait()


def relay_kernel(less_any, more_any, after_1, after_2, after_3, low_any, high_any, low_ref, high_ref, sems):
    half = PART // 2
    copies = [
        pltpu.make_async_copy(less_any.at[pl.ds(0, half)], low_ref, sems.at[0]),
        pltpu.make_async_copy(more_any.at[pl.ds(half, half)], high_ref, sems.at[1]),
    ]
    for copy in copies:
        copy.start()
    for copy in copies:
        copy.wait()
    copies = [
        pltpu.make_async_copy(low_ref, low_any, sems.at[0]),
        pltpu.make_async_copy(high_ref, high_any, sems.at[1]),
    ]
    for copy in copies:
        copy.start()
    for copy in copies:
        copy.wait()


def arrange_kernel(places, at_ref, *refs):
    pieces, (down_any, in_any, sems) = refs[: len(places)], refs[-3:]
    copies = []
    for i, (ref, (away, start)) in enumerate(zip(pieces, places)):
        q = lax.rem(at_ref[1] + away, GY)
        to = pl.ds(pl.multiple_of(q * PART + start, 32), ref.shape[0])
        copies.append(pltpu.make_async_copy(ref.at[:, pl.ds(0, HID)], down_any.at[to], sems.at[0, i]))
        copies.append(pltpu.make_async_copy(ref.at[:, pl.ds(HID, 2 * HID)], in_any.at[to], sems.at[1, i]))
    for copy in copies:
        copy.start()
    for copy in copies:
        copy.wait()


def order_kernel(pre_ref, after_ref, out_ref):
    row = iota((ROWS, ROWS), 0)
    col = iota((ROWS, ROWS), 1)
    swap_rows = one_hot(col == (row % N_EXP) * CAP + row // N_EXP)
    out_ref[...] = nn(swap_rows, pre_ref[...]).astype(BF)


def factor_kernel(pre_0, pre_1, pre_2, pre_3, factor_ref, act_ref, token_ref):
    for r, pre_ref in enumerate((pre_0, pre_1, pre_2, pre_3)):
        for s in range(CAP):
            span = slice(s * N_EXP, (s + 1) * N_EXP)
            gate_pre = pre_ref[span, :HID].astype(F32)
            up_pre = pre_ref[span, HID:].astype(F32)
            sig = jax.nn.sigmoid(gate_pre)
            lift = gate_pre * sig
            factor_ref[r, span, :HID] = (up_pre * sig * (1.0 + gate_pre * (1.0 - sig))).astype(BF)
            factor_ref[r, span, HID:] = lift.astype(BF)
            act_ref[r, span, :] = (lift * up_pre).astype(BF)
    token_ref[...] = jnp.zeros(token_ref.shape, F32)


def put_rows(split, block_of, sent_ref, r):
    for s in range(CAP):
        rows = from_pairs(block_of(slice(s * HALF, (s + 1) * HALF)))
        halves = nn(split, rows).astype(BF)
        span = slice(s * N_EXP, (s + 1) * N_EXP)
        sent_ref[r, span, :HALF] = halves[:N_EXP]
        sent_ref[r, span, HALF:] = halves[N_EXP:]


def hidden_kernel(
    at_ref, recv_any, down_any, part_any,
    recv_ref, down_ref, sent_ref, part_ref, in_sems, down_sem, out_sems,
):
    fetches = []
    for r in range(GX):
        span = pl.ds(lax.rem(at_ref[0] + (GX - r), GX) * N_EXP, N_EXP)
        fetches.append(pltpu.make_async_copy(recv_any.at[span], recv_ref.at[r], in_sems.at[r]))
    fetches.append(pltpu.make_async_copy(down_any, down_ref, down_sem))
    for copy in fetches:
        copy.start()
    split = split_halves()
    for r in range(GX):
        fetches[r].wait()
        put_rows(split, lambda cols: recv_ref[r, :, :, cols], sent_ref, r)
    fetches[GX].wait()
    copies = []
    for pair in range(2):
        sent = jnp.concatenate([sent_ref[2 * pair], sent_ref[2 * pair + 1]], axis=0)
        part = nn(sent, down_ref[...]).astype(BF)
        for r in (2 * pair, 2 * pair + 1):
            part_ref[r] = part[(r % 2) * ROWS : (r % 2 + 1) * ROWS]
            g = lax.rem(at_ref[0] + (GX - r), GX)
            copies.append(pltpu.make_async_copy(part_ref.at[r], part_any.at[g], out_sems.at[r]))
            copies[-1].start()
    for copy in copies:
        copy.wait()


def sum_kernel(part_ref, out_ref):
    total = part_ref[0].astype(F32) + part_ref[1].astype(F32)
    out_ref[...] = (total + (part_ref[2].astype(F32) + part_ref[3].astype(F32))).astype(BF)


def back_kernel(at_ref, hidden_ref, factor_ref, in_ref, msg_any, msg_ref, sems):
    grads = []
    for r in range(GX):
        hidden = hidden_ref[lax.rem(at_ref[0] + (GX - r), GX)].astype(F32)
        gate_grad = (hidden * factor_ref[r, :, :HID].astype(F32)).astype(BF)
        up_grad = (hidden * factor_ref[r, :, HID:].astype(F32)).astype(BF)
        grads.append(jnp.concatenate([gate_grad, up_grad], axis=1))
    rows = nt(jnp.concatenate(grads, axis=0), in_ref[...]).astype(BF)
    join = join_halves()
    copies = []
    for r in range(GX):
        g = lax.rem(at_ref[0] + (GX - r), GX)
        for s in range(CAP):
            own = rows[(r * CAP + s) * N_EXP : (r * CAP + s + 1) * N_EXP]
            both = jnp.concatenate([own[:, :HALF], own[:, HALF:]], axis=0)
            msg_ref[r, :, :, s * HALF : (s + 1) * HALF] = to_pairs(nn(join, both))
        span = pl.ds(g * N_EXP, N_EXP)
        copies.append(pltpu.make_async_copy(msg_ref.at[r], msg_any.at[span], sems.at[r]))
        copies[-1].start()
    for copy in copies:
        copy.wait()


def total_kernel(part_0, part_1, part_2, part_3, out_ref):
    total = part_0[...].astype(F32) + part_1[...].astype(F32)
    out_ref[...] = (total + (part_2[...].astype(F32) + part_3[...].astype(F32))).astype(BF)


def down_kernel(at_ref, recv_ref, act_ref, after_ref, out_0, out_1, out_2, out_3, sent_ref, full_ref):
    split = split_halves()
    for r in range(GX):
        span = pl.ds(lax.rem(at_ref[0] + (GX - r), GX) * N_EXP, N_EXP)
        put_rows(split, lambda cols: recv_ref[span, :, cols], sent_ref, r)
    sent = jnp.concatenate([sent_ref[r] for r in range(GX)], axis=0)
    act = jnp.concatenate([act_ref[r] for r in range(GX)], axis=0)
    full_ref[...] = tn(sent, act).astype(BF)
    for r, out_ref in enumerate((out_0, out_1, out_2, out_3)):
        q = lax.rem(at_ref[1] + r, GY)
        out_ref[...] = full_ref[pl.ds(pl.multiple_of(q * PART, 64), PART), :]


def gather_kernel(ret_ref, ids_ref, slots_ref, out_any, out_ref, sems):
    pick, _ = select(ids_ref, slots_ref, None)
    copies = []
    for g in range(GX):
        rows = jnp.concatenate(
            [
                from_pairs(ret_ref[g * N_EXP : (g + 1) * N_EXP, :, s * HALF : (s + 1) * HALF])
                for s in range(CAP)
            ],
            axis=0,
        )
        halves = tn(pick, rows).astype(BF)
        out_ref[g, :, :HALF] = halves[:TOK]
        out_ref[g, :, HALF:] = halves[TOK:]
        copies.append(
            pltpu.make_async_copy(out_ref.at[g], out_any.at[:, pl.ds(g * WIDE, WIDE)], sems.at[g])
        )
        copies[-1].start()
    for copy in copies:
        copy.wait()


def swap(value):
    return lax.all_to_all(value, ("gx", "expert"), 0, 0, tiled=True)


def swap_gx(value):
    return lax.all_to_all(value, "gx", 0, 0, tiled=True)


def step(value, axis, r):
    return lax.ppermute(value, axis, [(i, (i + r) % 4) for i in range(4)])


def steps(value, axis):
    return [step(value, axis, r) for r in range(1, 4)]


def per_device(out_grad, route_ids, route_slots, route_probs, saved_pre, w_gate, w_up, w_down):
    ids, slots, probs = route_ids.T, route_slots.T, route_probs.T
    at = jnp.stack([lax.axis_index("gx"), lax.axis_index("gy")])
    smem = pl.BlockSpec(memory_space=pltpu.SMEM)
    vmem = pl.BlockSpec(memory_space=pltpu.VMEM)
    anywhere = pl.BlockSpec(memory_space=pl.ANY)
    message = arr(GX * N_EXP, 2, CAP * HALF)

    msg, packed = call(
        pick_kernel,
        (message, arr(PART, 3 * HID)),
        1 << 29,
        1 << 23,
        VMEM_MOST,
        in_specs=[anywhere] * 7,
        out_specs=[anywhere] * 2,
        scratch_shapes=[
            pltpu.VMEM((GX, TOK, WIDE), BF),
            pltpu.VMEM(ids.shape, jnp.int32),
            pltpu.VMEM(ids.shape, jnp.int32),
            pltpu.VMEM(ids.shape, F32),
            pltpu.VMEM(message.shape, BF),
            pltpu.VMEM((PART, 3 * HID), BF),
            pltpu.SemaphoreType.DMA((GX,)),
            pltpu.SemaphoreType.DMA((3,)),
            pltpu.SemaphoreType.DMA((GX,)),
            pltpu.SemaphoreType.DMA((3,)),
            pltpu.SemaphoreType.DMA,
        ],
    )(out_grad, ids, slots, probs, w_down[0].T, w_gate[0], w_up[0])
    recv = swap(msg)

    pre = call(order_kernel, arr(ROWS, 2 * HID), 1 << 27, 1 << 21, in_specs=[vmem, anywhere])(
        saved_pre[0], msg
    )
    pres = steps(pre, "gx")
    less, more = step(packed, "gy", 1), step(packed, "gy", 3)
    half = arr(PART // 2, 3 * HID)
    low, high = call(
        relay_kernel,
        (half, half),
        0,
        1 << 22,
        in_specs=[anywhere] * 5,
        out_specs=[anywhere] * 2,
        scratch_shapes=[
            pltpu.VMEM(half.shape, BF),
            pltpu.VMEM(half.shape, BF),
            pltpu.SemaphoreType.DMA((2,)),
        ],
    )(less, more, *pres)
    factors, act, factors_done = call(
        factor_kernel,
        (arr(GX, ROWS, 2 * HID), arr(GX, ROWS, HID), arr(8, 128, dtype=F32)),
        1 << 25,
        1 << 23,
        VMEM_MOST,
    )(pre, *pres)
    def arrange(places, pieces, others, aliases):
        return call(
            functools.partial(arrange_kernel, places),
            (arr(WIDE, HID), arr(WIDE, 2 * HID)),
            0,
            1 << 24,
            VMEM_MOST,
            in_specs=[smem] + [vmem] * len(pieces) + [anywhere] * len(others),
            out_specs=[anywhere] * 2,
            scratch_shapes=[pltpu.SemaphoreType.DMA((2, len(places)))],
            input_output_aliases=aliases,
        )(at, *pieces, *others)

    near = arrange(((0, 0), (GY - 1, 0), (1, 0)), (packed, less, more), (), {})
    down_w, in_w = arrange(
        ((2, 0), (2, PART // 2)),
        (step(low, "gy", 1), step(high, "gy", 3)),
        (*near, factors_done),
        {3: 0, 4: 1},
    )

    part = call(
        hidden_kernel,
        arr(GX, ROWS, HID),
        1 << 31,
        1 << 23,
        VMEM_MOST,
        in_specs=[smem, anywhere, anywhere],
        out_specs=anywhere,
        scratch_shapes=[
            pltpu.VMEM((GX, N_EXP, 2, CAP * HALF), BF),
            pltpu.VMEM((WIDE, HID), BF),
            pltpu.VMEM((GX, ROWS, WIDE), BF),
            pltpu.VMEM((GX, ROWS, HID), BF),
            pltpu.SemaphoreType.DMA((GX,)),
            pltpu.SemaphoreType.DMA,
            pltpu.SemaphoreType.DMA((GX,)),
        ],
    )(at, recv, down_w)
    total = call(sum_kernel, arr(ROWS, HID), 0, 1 << 21)(swap_gx(part))
    hidden = lax.all_gather(total, "gx", axis=0)
    back = call(
        back_kernel,
        message,
        1 << 32,
        1 << 23,
        in_specs=[smem] + [vmem] * 3,
        out_specs=anywhere,
        scratch_shapes=[
            pltpu.VMEM((GX, N_EXP, 2, CAP * HALF), BF),
            pltpu.SemaphoreType.DMA((GX,)),
        ],
    )(at, hidden, factors, in_w)
    ret = swap(back)

    downs = call(
        down_kernel,
        (arr(PART, HID),) * GY,
        1 << 31,
        1 << 22,
        in_specs=[smem] + [vmem] * 2 + [anywhere],
        scratch_shapes=[pltpu.VMEM((GX, ROWS, WIDE), BF), pltpu.VMEM((WIDE, HID), BF)],
    )(at, recv, act, back)
    grad_down = call(total_kernel, arr(PART, HID), 0, 1 << 21)(
        downs[0], *[step(downs[r], "gy", r) for r in range(1, GY)]
    )
    input_grad = call(
        gather_kernel,
        arr(TOK, GX * WIDE),
        1 << 30,
        1 << 22,
        in_specs=[vmem] * 3,
        out_specs=anywhere,
        scratch_shapes=[pltpu.VMEM((GX, TOK, WIDE), BF), pltpu.SemaphoreType.DMA((GX,))],
    )(ret, ids, slots)
    return (input_grad, grad_down.T[None])


def solution(mesh):
    devices = mesh.devices
    grid = Mesh(devices.reshape((GX, GY) + devices.shape[1:]), ("gx", "gy", "expert"))
    rows = P(("gx", "gy", "expert"), None)
    return jax.shard_map(
        per_device,
        mesh=grid,
        in_specs=(
            rows,
            rows,
            rows,
            rows,
            P("expert", ("gx", "gy"), None),
            P("expert", ("gx", "gy"), None),
            P("expert", ("gx", "gy"), None),
            P("expert", None, ("gx", "gy")),
        ),
        out_specs=(rows, P("expert", None, ("gx", "gy"))),
        check_vma=False,
    )
```

```python
import functools

import jax
import jax.numpy as jnp
from jax import lax
from jax.experimental import pallas as pl
from jax.experimental.pallas import tpu as pltpu
from jax.sharding import Mesh, PartitionSpec as P

BF = jnp.bfloat16
F32 = jnp.float32

N_EXP = 32
CAP = 5
TOK = 128
GX = 4
GY = 4
WIDE = 1280
HALF = 640
HID = 768
ROWS = N_EXP * CAP
PAIRS = 2 * N_EXP
PART = 320
VMEM_LIMIT = 16 * 1024 * 1024
VMEM_MOST = 60 * 1024 * 1024


def iota(shape, dim):
    return lax.broadcasted_iota(jnp.int32, shape, dim)


def nn(left, right):
    return lax.dot_general(left, right, (((1,), (0,)), ((), ())), preferred_element_type=F32)


def nt(left, right):
    return lax.dot_general(left, right, (((1,), (1,)), ((), ())), preferred_element_type=F32)


def tn(left, right):
    return lax.dot_general(left, right, (((0,), (0,)), ((), ())), preferred_element_type=F32)


def one_hot(mask):
    return jnp.where(mask, 1.0, 0.0).astype(BF)


def call(body, out_shape, flops=0, moved=0, limit=VMEM_LIMIT, **kwargs):
    return pl.pallas_call(
        body,
        out_shape=out_shape,
        compiler_params=pltpu.CompilerParams(vmem_limit_bytes=limit),
        cost_estimate=pl.CostEstimate(flops=flops, bytes_accessed=moved, transcendentals=0),
        **kwargs,
    )


def arr(*dims, dtype=BF):
    return jax.ShapeDtypeStruct(dims, dtype)


def select(ids_ref, slots_ref, probs):
    code = ids_ref[...] * CAP + slots_ref[...]
    shape = (CAP * PAIRS, TOK)
    row = iota(shape, 0)
    row_code = ((row % PAIRS) // 2) * CAP + row // PAIRS
    hits = jnp.zeros(shape, F32)
    weight = jnp.zeros(shape, F32)
    for k in range(code.shape[0]):
        same = row_code == code[k : k + 1, :]
        hits = hits + jnp.where(same, 1.0, 0.0)
        if probs is not None:
            weight = weight + jnp.where(same, probs[k : k + 1, :], 0.0)
    lower = row % 2 == 0
    pick = jnp.concatenate([jnp.where(lower, hits, 0.0), jnp.where(lower, 0.0, hits)], axis=1)
    return pick.astype(BF), jnp.sum(weight, axis=1, keepdims=True)


def split_halves():
    row = iota((PAIRS, PAIRS), 0)
    col = iota((PAIRS, PAIRS), 1)
    return one_hot(col == (row % N_EXP) * 2 + row // N_EXP)


def join_halves():
    row = iota((PAIRS, PAIRS), 0)
    col = iota((PAIRS, PAIRS), 1)
    return one_hot(row == (col % N_EXP) * 2 + col // N_EXP)


def to_pairs(rows):
    return rows.astype(BF).reshape(N_EXP, 2, HALF)


def from_pairs(block):
    return block.reshape(PAIRS, HALF)


def pick_kernel(
    og_any, ids_any, slots_any, probs_any, down_any, gate_any, up_any,
    msg_any, packed_any,
    og_ref, ids_ref, slots_ref, probs_ref, msg_ref, packed_ref,
    og_sem, in_sem, out_sem, fetch_sem, store_sem,
):
    small = [
        pltpu.make_async_copy(src, dst, in_sem.at[i])
        for i, (src, dst) in enumerate(((ids_any, ids_ref), (slots_any, slots_ref), (probs_any, probs_ref)))
    ]
    wide = [
        pltpu.make_async_copy(og_any.at[:, pl.ds(g * WIDE, WIDE)], og_ref.at[g], og_sem.at[g])
        for g in range(GX)
    ]
    fetches = [
        pltpu.make_async_copy(src, packed_ref.at[:, pl.ds(i * HID, HID)], fetch_sem.at[i])
        for i, src in enumerate((down_any, gate_any, up_any))
    ]
    stores = [pltpu.make_async_copy(packed_ref, packed_any, store_sem)]
    for copy in small + wide + fetches:
        copy.start()
    for copy in small:
        copy.wait()
    pick, weight = select(ids_ref, slots_ref, probs_ref[...])
    sends = []
    for g in range(GX):
        wide[g].wait()
        both = jnp.concatenate([og_ref[g, :, :HALF], og_ref[g, :, HALF:]], axis=0)
        rows = nn(pick, both) * weight
        for s in range(CAP):
            msg_ref[g * N_EXP : (g + 1) * N_EXP, :, s * HALF : (s + 1) * HALF] = to_pairs(
                rows[s * PAIRS : (s + 1) * PAIRS]
            )
        span = pl.ds(g * N_EXP, N_EXP)
        sends.append(pltpu.make_async_copy(msg_ref.at[span], msg_any.at[span], out_sem.at[g]))
        sends[-1].start()
        if g == 1:
            for copy in fetches:
                copy.wait()
            for copy in stores:
                copy.start()
    for copy in sends + stores:
        copy.wait()


def relay_kernel(less_any, more_any, after_1, after_2, after_3, low_any, high_any, low_ref, high_ref, sems):
    half = PART // 2
    copies = [
        pltpu.make_async_copy(less_any.at[pl.ds(0, half)], low_ref, sems.at[0]),
        pltpu.make_async_copy(more_any.at[pl.ds(half, half)], high_ref, sems.at[1]),
    ]
    for copy in copies:
        copy.start()
    for copy in copies:
        copy.wait()
    copies = [
        pltpu.make_async_copy(low_ref, low_any, sems.at[0]),
        pltpu.make_async_copy(high_ref, high_any, sems.at[1]),
    ]
    for copy in copies:
        copy.start()
    for copy in copies:
        copy.wait()


def arrange_kernel(places, at_ref, *refs):
    pieces, (down_any, in_any, sems) = refs[: len(places)], refs[-3:]
    copies = []
    for i, (ref, (away, start)) in enumerate(zip(pieces, places)):
        q = lax.rem(at_ref[1] + away, GY)
        to = pl.ds(pl.multiple_of(q * PART + start, 32), ref.shape[0])
        copies.append(pltpu.make_async_copy(ref.at[:, pl.ds(0, HID)], down_any.at[to], sems.at[0, i]))
        copies.append(pltpu.make_async_copy(ref.at[:, pl.ds(HID, 2 * HID)], in_any.at[to], sems.at[1, i]))
    for copy in copies:
        copy.start()
    for copy in copies:
        copy.wait()


def order_kernel(pre_ref, after_ref, out_ref):
    row = iota((ROWS, ROWS), 0)
    col = iota((ROWS, ROWS), 1)
    swap_rows = one_hot(col == (row % N_EXP) * CAP + row // N_EXP)
    out_ref[...] = nn(swap_rows, pre_ref[...]).astype(BF)


def factor_kernel(pre_0, pre_1, pre_2, pre_3, factor_ref, act_ref, token_ref):
    for r, pre_ref in enumerate((pre_0, pre_1, pre_2, pre_3)):
        for s in range(CAP):
            span = slice(s * N_EXP, (s + 1) * N_EXP)
            gate_pre = pre_ref[span, :HID].astype(F32)
            up_pre = pre_ref[span, HID:].astype(F32)
            sig = jax.nn.sigmoid(gate_pre)
            lift = gate_pre * sig
            factor_ref[r, span, :HID] = (up_pre * sig * (1.0 + gate_pre * (1.0 - sig))).astype(BF)
            factor_ref[r, span, HID:] = lift.astype(BF)
            act_ref[r, span, :] = (lift * up_pre).astype(BF)
    token_ref[...] = jnp.zeros(token_ref.shape, F32)


def put_rows(split, block_of, sent_ref, r):
    for s in range(CAP):
        rows = from_pairs(block_of(slice(s * HALF, (s + 1) * HALF)))
        halves = nn(split, rows).astype(BF)
        span = slice(s * N_EXP, (s + 1) * N_EXP)
        sent_ref[r, span, :HALF] = halves[:N_EXP]
        sent_ref[r, span, HALF:] = halves[N_EXP:]


def hidden_kernel(
    at_ref, recv_any, down_any, part_any,
    recv_ref, down_ref, sent_ref, part_ref, in_sem, down_sem, out_sems,
):
    recv = pltpu.make_async_copy(recv_any, recv_ref, in_sem)
    down = pltpu.make_async_copy(down_any, down_ref, down_sem)
    recv.start()
    down.start()
    split = split_halves()
    recv.wait()
    for r in range(GX):
        span = pl.ds(lax.rem(at_ref[0] + (GX - r), GX) * N_EXP, N_EXP)
        put_rows(split, lambda cols: recv_ref[span, :, cols], sent_ref, r)
    down.wait()
    copies = []
    for pair in range(2):
        sent = jnp.concatenate([sent_ref[2 * pair], sent_ref[2 * pair + 1]], axis=0)
        part = nn(sent, down_ref[...]).astype(BF)
        for r in (2 * pair, 2 * pair + 1):
            part_ref[r] = part[(r % 2) * ROWS : (r % 2 + 1) * ROWS]
            g = lax.rem(at_ref[0] + (GX - r), GX)
            copies.append(pltpu.make_async_copy(part_ref.at[r], part_any.at[g], out_sems.at[r]))
            copies[-1].start()
    for copy in copies:
        copy.wait()


def sum_kernel(part_ref, out_ref):
    total = part_ref[0].astype(F32) + part_ref[1].astype(F32)
    out_ref[...] = (total + (part_ref[2].astype(F32) + part_ref[3].astype(F32))).astype(BF)


def back_kernel(at_ref, hidden_ref, factor_ref, in_ref, msg_any, msg_ref, sems):
    grads = []
    for r in range(GX):
        hidden = hidden_ref[lax.rem(at_ref[0] + (GX - r), GX)].astype(F32)
        gate_grad = (hidden * factor_ref[r, :, :HID].astype(F32)).astype(BF)
        up_grad = (hidden * factor_ref[r, :, HID:].astype(F32)).astype(BF)
        grads.append(jnp.concatenate([gate_grad, up_grad], axis=1))
    rows = nt(jnp.concatenate(grads, axis=0), in_ref[...]).astype(BF)
    join = join_halves()
    copies = []
    for r in range(GX):
        g = lax.rem(at_ref[0] + (GX - r), GX)
        for s in range(CAP):
            own = rows[(r * CAP + s) * N_EXP : (r * CAP + s + 1) * N_EXP]
            both = jnp.concatenate([own[:, :HALF], own[:, HALF:]], axis=0)
            msg_ref[r, :, :, s * HALF : (s + 1) * HALF] = to_pairs(nn(join, both))
        span = pl.ds(g * N_EXP, N_EXP)
        copies.append(pltpu.make_async_copy(msg_ref.at[r], msg_any.at[span], sems.at[r]))
        copies[-1].start()
    for copy in copies:
        copy.wait()


def total_kernel(part_0, part_1, part_2, part_3, out_ref):
    total = part_0[...].astype(F32) + part_1[...].astype(F32)
    out_ref[...] = (total + (part_2[...].astype(F32) + part_3[...].astype(F32))).astype(BF)


def down_kernel(at_ref, recv_ref, act_ref, after_ref, out_0, out_1, out_2, out_3, sent_ref, full_ref):
    split = split_halves()
    for r in range(GX):
        span = pl.ds(lax.rem(at_ref[0] + (GX - r), GX) * N_EXP, N_EXP)
        put_rows(split, lambda cols: recv_ref[span, :, cols], sent_ref, r)
    sent = jnp.concatenate([sent_ref[r] for r in range(GX)], axis=0)
    act = jnp.concatenate([act_ref[r] for r in range(GX)], axis=0)
    full_ref[...] = tn(sent, act).astype(BF)
    for r, out_ref in enumerate((out_0, out_1, out_2, out_3)):
        q = lax.rem(at_ref[1] + r, GY)
        out_ref[...] = full_ref[pl.ds(pl.multiple_of(q * PART, 64), PART), :]


def gather_kernel(ret_ref, ids_ref, slots_ref, out_any, out_ref, sems):
    pick, _ = select(ids_ref, slots_ref, None)
    copies = []
    for g in range(GX):
        rows = jnp.concatenate(
            [
                from_pairs(ret_ref[g * N_EXP : (g + 1) * N_EXP, :, s * HALF : (s + 1) * HALF])
                for s in range(CAP)
            ],
            axis=0,
        )
        halves = tn(pick, rows).astype(BF)
        out_ref[g, :, :HALF] = halves[:TOK]
        out_ref[g, :, HALF:] = halves[TOK:]
        copies.append(
            pltpu.make_async_copy(out_ref.at[g], out_any.at[:, pl.ds(g * WIDE, WIDE)], sems.at[g])
        )
        copies[-1].start()
    for copy in copies:
        copy.wait()


def swap(value):
    return lax.all_to_all(value, ("gx", "expert"), 0, 0, tiled=True)


def swap_gx(value):
    return lax.all_to_all(value, "gx", 0, 0, tiled=True)


def step(value, axis, r):
    return lax.ppermute(value, axis, [(i, (i + r) % 4) for i in range(4)])


def steps(value, axis):
    return [step(value, axis, r) for r in range(1, 4)]


def per_device(out_grad, route_ids, route_slots, route_probs, saved_pre, w_gate, w_up, w_down):
    ids, slots, probs = route_ids.T, route_slots.T, route_probs.T
    at = jnp.stack([lax.axis_index("gx"), lax.axis_index("gy")])
    smem = pl.BlockSpec(memory_space=pltpu.SMEM)
    vmem = pl.BlockSpec(memory_space=pltpu.VMEM)
    anywhere = pl.BlockSpec(memory_space=pl.ANY)
    message = arr(GX * N_EXP, 2, CAP * HALF)

    msg, packed = call(
        pick_kernel,
        (message, arr(PART, 3 * HID)),
        1 << 29,
        1 << 23,
        VMEM_MOST,
        in_specs=[anywhere] * 7,
        out_specs=[anywhere] * 2,
        scratch_shapes=[
            pltpu.VMEM((GX, TOK, WIDE), BF),
            pltpu.VMEM(ids.shape, jnp.int32),
            pltpu.VMEM(ids.shape, jnp.int32),
            pltpu.VMEM(ids.shape, F32),
            pltpu.VMEM(message.shape, BF),
            pltpu.VMEM((PART, 3 * HID), BF),
            pltpu.SemaphoreType.DMA((GX,)),
            pltpu.SemaphoreType.DMA((3,)),
            pltpu.SemaphoreType.DMA((GX,)),
            pltpu.SemaphoreType.DMA((3,)),
            pltpu.SemaphoreType.DMA,
        ],
    )(out_grad, ids, slots, probs, w_down[0].T, w_gate[0], w_up[0])
    recv = swap(msg)

    pre = call(order_kernel, arr(ROWS, 2 * HID), 1 << 27, 1 << 21, in_specs=[vmem, anywhere])(
        saved_pre[0], msg
    )
    pres = steps(pre, "gx")
    less, more = step(packed, "gy", 1), step(packed, "gy", 3)
    half = arr(PART // 2, 3 * HID)
    low, high = call(
        relay_kernel,
        (half, half),
        0,
        1 << 22,
        in_specs=[anywhere] * 5,
        out_specs=[anywhere] * 2,
        scratch_shapes=[
            pltpu.VMEM(half.shape, BF),
            pltpu.VMEM(half.shape, BF),
            pltpu.SemaphoreType.DMA((2,)),
        ],
    )(less, more, *pres)
    factors, act, factors_done = call(
        factor_kernel,
        (arr(GX, ROWS, 2 * HID), arr(GX, ROWS, HID), arr(8, 128, dtype=F32)),
        1 << 25,
        1 << 23,
        VMEM_MOST,
    )(pre, *pres)
    def arrange(places, pieces, others, aliases):
        return call(
            functools.partial(arrange_kernel, places),
            (arr(WIDE, HID), arr(WIDE, 2 * HID)),
            0,
            1 << 24,
            VMEM_MOST,
            in_specs=[smem] + [vmem] * len(pieces) + [anywhere] * len(others),
            out_specs=[anywhere] * 2,
            scratch_shapes=[pltpu.SemaphoreType.DMA((2, len(places)))],
            input_output_aliases=aliases,
        )(at, *pieces, *others)

    near = arrange(((0, 0), (GY - 1, 0), (1, 0)), (packed, less, more), (), {})
    down_w, in_w = arrange(
        ((2, 0), (2, PART // 2)),
        (step(low, "gy", 1), step(high, "gy", 3)),
        (*near, factors_done),
        {3: 0, 4: 1},
    )

    part = call(
        hidden_kernel,
        arr(GX, ROWS, HID),
        1 << 31,
        1 << 23,
        VMEM_MOST,
        in_specs=[smem, anywhere, anywhere],
        out_specs=anywhere,
        scratch_shapes=[
            pltpu.VMEM(message.shape, BF),
            pltpu.VMEM((WIDE, HID), BF),
            pltpu.VMEM((GX, ROWS, WIDE), BF),
            pltpu.VMEM((GX, ROWS, HID), BF),
            pltpu.SemaphoreType.DMA,
            pltpu.SemaphoreType.DMA,
            pltpu.SemaphoreType.DMA((GX,)),
        ],
    )(at, recv, down_w)
    total = call(sum_kernel, arr(ROWS, HID), 0, 1 << 21)(swap_gx(part))
    hidden = lax.all_gather(total, "gx", axis=0)
    back = call(
        back_kernel,
        message,
        1 << 32,
        1 << 23,
        in_specs=[smem] + [vmem] * 3,
        out_specs=anywhere,
        scratch_shapes=[
            pltpu.VMEM((GX, N_EXP, 2, CAP * HALF), BF),
            pltpu.SemaphoreType.DMA((GX,)),
        ],
    )(at, hidden, factors, in_w)
    ret = swap(back)

    downs = call(
        down_kernel,
        (arr(PART, HID),) * GY,
        1 << 31,
        1 << 22,
        in_specs=[smem] + [vmem] * 2 + [anywhere],
        scratch_shapes=[pltpu.VMEM((GX, ROWS, WIDE), BF), pltpu.VMEM((WIDE, HID), BF)],
    )(at, recv, act, back)
    grad_down = call(total_kernel, arr(PART, HID), 0, 1 << 21)(
        downs[0], *[step(downs[r], "gy", r) for r in range(1, GY)]
    )
    input_grad = call(
        gather_kernel,
        arr(TOK, GX * WIDE),
        1 << 30,
        1 << 22,
        in_specs=[vmem] * 3,
        out_specs=anywhere,
        scratch_shapes=[pltpu.VMEM((GX, TOK, WIDE), BF), pltpu.SemaphoreType.DMA((GX,))],
    )(ret, ids, slots)
    return (input_grad, grad_down.T[None])


def solution(mesh):
    devices = mesh.devices
    grid = Mesh(devices.reshape((GX, GY) + devices.shape[1:]), ("gx", "gy", "expert"))
    rows = P(("gx", "gy", "expert"), None)
    return jax.shard_map(
        per_device,
        mesh=grid,
        in_specs=(
            rows,
            rows,
            rows,
            rows,
            P("expert", ("gx", "gy"), None),
            P("expert", ("gx", "gy"), None),
            P("expert", ("gx", "gy"), None),
            P("expert", None, ("gx", "gy")),
        ),
        out_specs=(rows, P("expert", None, ("gx", "gy"))),
        check_vma=False,
    )
```
